256 devices in a mesh: leaf: 256 (over x, z, y, core).
Axes of the slice: x: 4, y: 4, z: 8, core: 2. Of those that a mesh axis runs over, the one named last changes fastest.
Arguments:
- rhs: float32 [16, 1048576], P(None, 'leaf'), may hold values from -6 to 6
- order: int32 [256, 4096], P('leaf'), may hold values from 0 to 4095, each once within a row
- leaf_basis: float32 [16384, 4096], P('leaf'), may hold values from -0.75 to 0.75
- near_pick: int32 [3, 16384], P(None, 'leaf'), may hold values from -1 to 1
- near_block: float32 [3, 16384, 4096], P(None, 'leaf'), may hold values from -0.4375 to 0.4375
- trans_one: float32 [16384, 4096], P('leaf'), may hold values from -0.5 to 0.5
- trans_two: float32 [8192, 4096], P('leaf'), may hold values from -0.5 to 0.5
- trans_root: float32 [4096, 4096], P('leaf'), may hold values from -0.1875 to 0.1875
- far_pick_a: int32 [3, 16384], P(None, 'leaf'), may hold values from 0 to 3
- far_block_a: float32 [3, 16384, 4096], P(None, 'leaf'), may hold values from -0.4375 to 0.4375
- far_pick_b: int32 [3, 8192], P(None, 'leaf'), may hold values from 0 to 3
- far_block_b: float32 [3, 8192, 4096], P(None, 'leaf'), may hold values from -0.4375 to 0.4375
- far_pick_c: int32 [3, 4096], P(None, 'leaf'), may hold values from 0 to 3
- far_block_c: float32 [3, 4096, 4096], P(None, 'leaf'), may hold values from -0.4375 to 0.4375
- top_transfer: float32 [3, 256, 4096], P(None, 'leaf'), may hold values from -1 to 1, as said below
- top_source: int32 [1024], P('leaf'), may hold values from 0 to 31
- top_target: int32 [1024], P('leaf'), may hold values from 0 to 31
- top_block: float32 [1024, 4096], P('leaf'), may hold values from -0.75 to 0.75
Outputs:
- product_out: float32 [16, 1048576], P(None, 'leaf')
The draws below stay inside these ranges and needn't reach their ends.
Inputs may be any that keep to these rules, and one draw needn't show every extreme that they name: `top_transfer`: entry [j, d] equals entry [j, d - d % 2^j].
All inputs are finite; a program needn't handle non-finite values.
Results may differ from the reference program's by a relative error of at most 0.0001.
Values sent between devices are 32-bit elements; how exact they have to be, the bound alone decides.
A program may use at most 128 MiB of HBM per device.

```python
import jax
import jax.numpy as jnp
from jax import lax

LEAF = 64
RANK = 64
NRHS = 16
L_DEV = 64
SLOTS = 3
NEAR = 3
TOPL = 3
PTS_DEV = 4096
DEVS = 256
NPTS = 1048576
LEAVES = 16384
NTOP = 32
TOPBLK = 1024


def draw_top_transfer(key, part):
    key = jax.random.fold_in(key, 11)
    bound_value = (1.5 / RANK) ** 0.5
    fresh_draw = jax.random.uniform(key, (TOPL, DEVS, RANK * RANK), jnp.float32, -bound_value, bound_value)
    stacked = []
    for height in range(TOPL):
        leaders = jnp.arange(DEVS) // 2 ** height * 2 ** height
        stacked.append(jnp.take(fresh_draw[height], leaders, axis=0))
    return jnp.stack(stacked)


def set_ends(values, key, least, largest):
    shape = values.shape
    spot = [jax.random.randint(jax.random.fold_in(key, axis), (), 0, shape[axis]) for axis in range(len(shape))]
    values = values.at[tuple(spot)].set(least)
    longest = shape.index(max(shape))
    spot[longest] = (spot[longest] + 1) % shape[longest]
    return values.at[tuple(spot)].set(largest)


def level_of(stream_key, extent, split, least, high):
    loudness, own = 1.0, jax.random.fold_in(stream_key, 6)
    for dim, blocks in split:
        heights = jnp.exp(jax.random.uniform(jax.random.fold_in(own, dim), (blocks,), jnp.float32, least / len(split), high / len(split)))
        loudness = loudness * jnp.repeat(heights, extent[dim] // blocks).reshape([-1 if axis == dim else 1 for axis in range(len(extent))])
    return loudness


def bell_draw(key, shape, spread, bound, shards=(), held_as=jnp.bfloat16):
    drawn = spread * jax.random.normal(key, shape, jnp.float32)
    if shards:
        drawn = drawn * level_of(key, shape, shards, -0.22, 0.18)
    return jnp.clip(drawn, -bound, bound).astype(held_as)


def setup_inputs(seed: int = 0) -> dict:
    arg_keys = jax.random.split(jax.random.key(seed), 19)
    return {
        "rhs": bell_draw(arg_keys[0], (NRHS, NPTS), 1.0, 6.0, ((1, 256),), jnp.float32),
        "order": jax.vmap(lambda own: jax.random.permutation(own, PTS_DEV))(jax.random.split(arg_keys[1], DEVS)).reshape((DEVS, PTS_DEV)).astype(jnp.int32),
        "leaf_basis": bell_draw(arg_keys[2], (LEAVES, LEAF * RANK), LEAF ** -0.5, 0.75, ((0, 256),), jnp.float32),
        "near_pick": set_ends(jax.random.randint(arg_keys[3], (NEAR, LEAVES), -1, 2), jax.random.fold_in(arg_keys[3], 1), -1, 1).astype(jnp.int32),
        "near_block": bell_draw(arg_keys[4], (NEAR, LEAVES, LEAF * LEAF), (3 * LEAF) ** -0.5, 0.4375, ((1, 256),), jnp.float32),
        "trans_one": bell_draw(arg_keys[5], (LEAVES, RANK * RANK), (2 * RANK) ** -0.5, 0.5, ((0, 256),), jnp.float32),
        "trans_two": bell_draw(arg_keys[6], (LEAVES // 2, RANK * RANK), (2 * RANK) ** -0.5, 0.5, ((0, 256),), jnp.float32),
        "trans_root": bell_draw(arg_keys[7], (LEAVES // 4, RANK * RANK), (L_DEV // 4 * RANK) ** -0.5, 0.1875, ((0, 256),), jnp.float32),
        "far_pick_a": set_ends(jax.random.randint(arg_keys[8], (SLOTS, LEAVES), 0, 4), jax.random.fold_in(arg_keys[8], 1), 0, 3).astype(jnp.int32),
        "far_block_a": bell_draw(arg_keys[9], (SLOTS, LEAVES, RANK * RANK), (3 * RANK) ** -0.5, 0.4375, ((1, 256),), jnp.float32),
        "far_pick_b": set_ends(jax.random.randint(arg_keys[10], (SLOTS, LEAVES // 2), 0, 4), jax.random.fold_in(arg_keys[10], 1), 0, 3).astype(jnp.int32),
        "far_block_b": bell_draw(arg_keys[11], (SLOTS, LEAVES // 2, RANK * RANK), (3 * RANK) ** -0.5, 0.4375, ((1, 256),), jnp.float32),
        "far_pick_c": set_ends(jax.random.randint(arg_keys[12], (SLOTS, LEAVES // 4), 0, 4), jax.random.fold_in(arg_keys[12], 1), 0, 3).astype(jnp.int32),
        "far_block_c": bell_draw(arg_keys[13], (SLOTS, LEAVES // 4, RANK * RANK), (3 * RANK) ** -0.5, 0.4375, ((1, 256),), jnp.float32),
        "top_transfer": draw_top_transfer(jax.random.fold_in(arg_keys[18], 71), 0),
        "top_source": set_ends(jax.random.randint(arg_keys[15], (TOPBLK,), 0, NTOP), jax.random.fold_in(arg_keys[15], 1), 0, NTOP - 1).astype(jnp.int32),
        "top_target": set_ends(jax.random.randint(arg_keys[16], (TOPBLK,), 0, NTOP), jax.random.fold_in(arg_keys[16], 1), 0, NTOP - 1).astype(jnp.int32),
        "top_block": bell_draw(arg_keys[17], (TOPBLK, RANK * RANK), RANK ** -0.5, 0.75, ((0, 256),), jnp.float32),
    }


exactly = lax.Precision.HIGHEST


def product(form, first, second):
    return jnp.einsum(form, first, second, precision=exactly)


def square(flat, rows_count, cols_count):
    return flat.reshape(flat.shape[:-1] + (rows_count, cols_count))


def ascend(transfer, coeffs):
    carried = product('njk,jrn->krn', square(transfer, RANK, RANK), coeffs)
    return carried.reshape(coeffs.shape[0], coeffs.shape[1], -1, 2).sum(-1)


def descend(transfer, parents, fanout):
    return product('nkj,jrn->krn', square(transfer, RANK, RANK), jnp.repeat(parents, fanout, axis=2))


def far_term(picks, blocks, padded, node_count):
    offsets = jnp.where(picks < 2, picks - 3, picks)
    result = jnp.zeros((padded.shape[0], padded.shape[1], node_count), jnp.float32)
    for which_slot in range(picks.shape[0]):
        indices = (jnp.arange(node_count, dtype=jnp.int32) + offsets[which_slot] + 3).astype(jnp.int32)
        source = jnp.take(padded, indices, axis=2)
        result = result + product('nkj,jrn->krn', square(blocks[which_slot], RANK, RANK), source)
    return result


def near_term(picks, blocks, padded, node_count):
    result = jnp.zeros((padded.shape[0], node_count, padded.shape[2]), jnp.float32)
    for which_slot in range(picks.shape[0]):
        indices = (jnp.arange(node_count, dtype=jnp.int32) + picks[which_slot] + 1).astype(jnp.int32)
        source = jnp.take(padded, indices, axis=1)
        result = result + product('npq,rnq->rnp', square(blocks[which_slot], LEAF, LEAF), source)
    return result


def pad_nodes(coeffs):
    return jnp.pad(coeffs, ((0, 0), (0, 0), (3, 3)))


def reference(rhs, order, leaf_basis, near_pick, near_block, trans_one, trans_two, trans_root, far_pick_a, far_block_a, far_pick_b, far_block_b, far_pick_c, far_block_c, top_transfer, top_source, top_target, top_block):
    columns = rhs.shape[0]
    leaves = leaf_basis.shape[0]
    devices, per_device = order.shape
    basis = square(leaf_basis, LEAF, RANK)
    grouped = rhs.reshape(columns, devices, per_device)
    ordered = jnp.take_along_axis(grouped, order[None], axis=2).reshape(columns, leaves, LEAF)
    level_zero = product('npk,rnp->krn', basis, ordered)
    level_one = ascend(trans_one, level_zero)
    level_two = ascend(trans_two, level_one)
    fanout = leaves // devices // 4
    rooted = product('njk,jrn->krn', square(trans_root, RANK, RANK), level_two).reshape(RANK, columns, devices, fanout).sum(-1)
    climbing = product('njk,jrn->krn', square(top_transfer[0], RANK, RANK), rooted)
    for height in range(1, TOPL):
        summed = climbing.reshape(RANK, columns, -1, 2).sum(-1)
        climbing = product('njk,jrn->krn', square(top_transfer[height][::2 ** height], RANK, RANK), summed)
    top_coeffs = climbing.reshape(RANK, columns, -1, 2).sum(-1)
    picked = top_coeffs[:, :, top_source]
    coupled = product('bkj,jrb->krb', square(top_block, RANK, RANK), picked)
    falling = jnp.zeros_like(top_coeffs).at[:, :, top_target].add(coupled)
    for height in range(TOPL - 1, -1, -1):
        falling = descend(top_transfer[height][::2 ** height], falling, 2)
    down_two = far_term(far_pick_c, far_block_c, pad_nodes(level_two), leaves // 4) + descend(trans_root, falling, fanout)
    down_one = far_term(far_pick_b, far_block_b, pad_nodes(level_one), leaves // 2) + descend(trans_two, down_two, 2)
    down_zero = far_term(far_pick_a, far_block_a, pad_nodes(level_zero), leaves) + descend(trans_one, down_one, 2)
    padded_rows = jnp.pad(ordered, ((0, 0), (1, 1), (0, 0)))
    values = product('npk,krn->rnp', basis, down_zero) + near_term(near_pick, near_block, padded_rows, leaves)
    inverse = jnp.argsort(order, axis=1).astype(jnp.int32)
    restored = jnp.take_along_axis(values.reshape(columns, devices, per_device), inverse[None], axis=2)
    return restored.reshape(columns, devices * per_device)
```

```python
import functools

import jax
import jax.numpy as jnp
from jax import lax
from jax.experimental import pallas as pl
from jax.experimental.pallas import tpu as pltpu
from jax.sharding import PartitionSpec as P

F32, BF16, I32 = jnp.float32, jnp.bfloat16, jnp.int32
MESH = pl.DeviceIdType.MESH
EXACT = lax.Precision.HIGHEST
NEAR_UNROLL = 2
UP_UNROLL = 8


def iota(shape, dim):
    return lax.broadcasted_iota(I32, shape, dim)


def dot(a, b, precision=None):
    return lax.dot_general(
        a, b, (((1,), (0,)), ((), ())), precision=precision, preferred_element_type=F32
    )


def dot_nt(a, b, precision=None):
    return lax.dot_general(
        a, b, (((1,), (1,)), ((), ())), precision=precision, preferred_element_type=F32
    )


def split(x):
    head = x.astype(BF16)
    return head, (x - head.astype(F32)).astype(BF16)


def low_half(rows):
    return iota((rows, 128), 1) < 64


def swap(x):
    return pltpu.roll(x, 64, 1)


def prepare(block):
    a = jnp.concatenate([block[:, 128 * c : 128 * c + 128] for c in range(32)], axis=0)
    rest = a - a.astype(BF16).astype(F32)
    low = low_half(256)
    first = jnp.where(low, a, rest)
    second = swap(jnp.where(low, rest, a))
    top = jnp.where(low, first, second)
    bottom = jnp.where(low, second, first)
    return jnp.concatenate([top, bottom], axis=0).astype(BF16)


def pack(block):
    return jnp.where(low_half(8), block[0:8], block[8:16])


def unpack(packed):
    low, other = low_half(8), swap(packed)
    return jnp.concatenate(
        [jnp.where(low, packed, other), jnp.where(low, other, packed)], axis=0
    )


def pair(tile):
    low, other = low_half(16), swap(tile)
    return jnp.where(low, tile, other), jnp.where(low, other, tile)


def e_rows(block):
    head, rest = split(block)
    return jnp.concatenate([head, rest], axis=1)


def pick_diagonal(wide, nodes):
    lane_node = iota((16, 512), 1) & 7
    result = wide[0:16]
    for n in range(1, nodes):
        result = jnp.where(lane_node == n, wide[16 * n : 16 * n + 16], result)
    return result


def table_of(tiles):
    head, rest = split(jnp.concatenate(tiles, axis=0))
    return jnp.concatenate([head, rest], axis=1)


def lookup(table, tile_index, lane_index):
    width = lane_index.shape[1]
    hot = jnp.where(iota((128, width), 0) == lane_index, 1.0, 0.0).astype(BF16)
    found = dot(table, jnp.concatenate([hot, hot], axis=0))
    tile_index = jnp.broadcast_to(tile_index, (16, width))
    result = found[0:16]
    for s in range(1, 32):
        result = jnp.where(tile_index == s, found[16 * s : 16 * s + 16], result)
    return result


def find_points(order, inverse):
    def step(j, total):
        row = order[:, pl.ds(pl.multiple_of(j * 512, 512), 512)]
        lane = iota((1, 512), 1)
        n, p = lane >> 6, lane & 63
        parity, c = p & 1, p >> 1
        tile = (j * 4 + parity * 2 + (c >> 4)).astype(F32)
        place = ((c & 15) * 8 + n).astype(F32)
        chosen = iota((32, 512), 0) == (row >> 7)
        rows = jnp.concatenate(
            [jnp.where(chosen, tile, 0.0), jnp.where(chosen, place, 0.0)], axis=0
        ).astype(BF16)
        columns = jnp.where(iota((128, 512), 0) == (row & 127), 1.0, 0.0).astype(BF16)
        return total + dot_nt(rows, columns)

    inverse[...] = lax.fori_loop(0, 8, step, jnp.zeros((64, 128), F32), unroll=2).astype(I32)


def times(lhs_terms, w_terms):
    lhs = jnp.concatenate(lhs_terms, axis=1)
    w = jnp.concatenate([w for term in w_terms for w in (term, term)], axis=1)
    return dot_nt(lhs, w)


def kernel(
    devices,
    rhs_h, order_h, lb_h, near_pick, near_h, t1_h, t2_h, tr_h,
    pick_a, fa_h, pick_b, fb_h, pick_c, fc_h, tt_h, top_source, top_target, tb_h,
    vals, inverse,
    rhs_v, order_v, lb_v, near_v, t1_v, t2_v, tr_v, fa_v, fb_v, fc_v, tt_v, tb4_v,
    tb_v, w_lb, w_t1, w_t2, w_tr, to_d, to_n, diagonal, dmat, table, tiles,
    e_ord, e0, e1, e2, e_down, near_f, far_a, far_b, far_c,
    t_rows, halo_up, halo_down, from_below, from_above,
    a_send, a_buf, b_send, b_buf, c_send, c_buf, d_send, d_buf,
    load_sem, halo_sems, a_ssem, a_rsem, b_ssem, b_rsem, c_ssem, c_rsem, d_ssem, d_rsem,
):
    me = lax.axis_index("leaf")
    count = devices // 8
    inside, group = me & 7, me >> 3
    base = me - inside
    above, below = (me + 1) & (devices - 1), (me + devices - 1) & (devices - 1)
    deep = min(8, count)
    wide = count // deep
    line, depth = group // deep, group & (deep - 1)

    def hops(offset):
        dx, dz = offset
        return min(dx, wide - dx) + min(dz, deep - dz)

    offsets = sorted(((dx, dz) for dx in range(wide) for dz in range(deep)), key=hops)[::-1]
    offsets = [(0, 0)] + offsets[:-1]

    def group_at(q, sign=1):
        dx, dz = offsets[q]
        dx, dz = (dx, dz) if sign > 0 else (wide - dx, deep - dz)
        return ((line + dx) & (wide - 1)) * deep + ((depth + dz) & (deep - 1))

    def mate(q):
        return base + ((inside + q) & 7)

    def far_mate(q):
        return group_at(q) * 8 + inside

    loads = {}
    for number, (name, src, dst) in enumerate(
        (
            ("order", order_h, order_v),
            ("rhs", rhs_h, rhs_v),
            ("lb", lb_h, lb_v),
            ("t1", t1_h, t1_v),
            ("t2", t2_h, t2_v),
            ("tr", tr_h, tr_v),
            ("tt", tt_h, tt_v),
            ("near", near_h, near_v),
            ("tb", tb_h, tb4_v),
            ("fa", fa_h, fa_v),
            ("fb", fb_h, fb_v),
            ("fc", fc_h, fc_v),
        )
    ):
        loads[name] = pltpu.make_async_copy(src, dst, load_sem.at[number])
        loads[name].start()

    barrier = pltpu.get_barrier_semaphore()

    def greet(device):
        pl.semaphore_signal(barrier, inc=1, device_id=(device,), device_id_type=MESH)

    greet(above)
    greet(below)

    @pl.loop(1, 8)
    def _(q):
        greet(mate(q))

    for q in range(1, count):
        greet(far_mate(q))

    n_lane, d_lane = iota((512, 512), 0), iota((512, 512), 1)
    wanted = (d_lane & 7) * 64 + ((d_lane >> 3) & 31) * 2 + (d_lane >> 8)
    to_d[...] = jnp.where(n_lane == wanted, 1.0, 0.0).astype(BF16)
    wanted = (n_lane & 7) * 64 + ((n_lane >> 3) & 31) * 2 + (n_lane >> 8)
    to_n[...] = jnp.where(d_lane == wanted, 1.0, 0.0).astype(BF16)
    diagonal[...] = jnp.where(
        (iota((128, 512), 1) & 7) == (iota((128, 512), 0) >> 4), 1.0, 0.0
    ).astype(BF16)

    loads["rhs"].wait()
    table[...] = table_of([rhs_v[:, 128 * t : 128 * t + 128] for t in range(32)])
    for name in ("order", "lb", "t1", "t2", "tr", "tt"):
        loads[name].wait()

    def group_of(ref, g):
        return ref[pl.ds(pl.multiple_of(g * 8, 8), 8), :]

    for j in range(8):
        row = order_v[:, 512 * j : 512 * j + 512]
        found = lookup(table[...], row >> 7, row & 127)
        for i in range(4):
            tile = found[:, 128 * i : 128 * i + 128]
            tiles[4 * j + i] = tile
            for k, block in enumerate(pair(tile)):
                e_ord[8 * j + 2 * i + k + 1] = e_rows(block)
        w_lb[j] = prepare(group_of(lb_v, j))
        w_t1[j] = prepare(group_of(t1_v, j))
        if j < 4:
            w_t2[j] = prepare(group_of(t2_v, j))
        if j < 2:
            w_tr[j] = prepare(group_of(tr_v, j))

    for j in range(3):
        for c in range(32):
            t_rows[j, c : c + 1, :] = tt_v[j, :, 128 * c : 128 * c + 128]
    sort = jnp.where(
        iota((64, 64), 0) == (iota((64, 64), 1) & 31) * 2 + (iota((64, 64), 1) >> 5), 1.0, 0.0
    ).astype(F32)

    def top_matrix(j):
        rows = t_rows[j]
        return dot(sort, jnp.concatenate([rows[:, :64], rows[:, 64:]], axis=0), EXACT)

    lift = dot(top_matrix(0), dot(top_matrix(1), top_matrix(2), EXACT), EXACT)
    lift_wide = jnp.concatenate([lift, lift], axis=1)
    lift_tall = jnp.concatenate([lift, lift], axis=0)

    def spread_rows(groups):
        x = jnp.concatenate(
            [
                jnp.concatenate([tiles[4 * g + i] for i in range(4)], axis=1)
                for g in range(groups)
            ],
            axis=0,
        )
        head, rest = split(x)
        rows = groups * 16
        moved = dot(jnp.concatenate([head, rest], axis=0), to_d[...]).astype(BF16)
        dmat[0, 0:rows, :] = moved[0:rows]
        dmat[1, 0:rows, :] = moved[rows:]

    def up_group(g, w):
        at = pl.ds(pl.multiple_of(g * 16, 16), 16)
        mask = diagonal[...]
        lhs = jnp.concatenate(
            [
                jnp.concatenate([dmat[0, at, :]] * 8, axis=0) * mask,
                jnp.concatenate([dmat[1, at, :]] * 8, axis=0) * mask,
            ],
            axis=0,
        )
        product = dot(lhs, w)
        both = product[0:128] + product[128:256]
        return both + swap(both)

    def each(groups, unroll, step):
        def body(g, carry):
            step(g)
            return carry

        lax.fori_loop(0, groups, body, 0, unroll=min(unroll, groups))

    halo_down[0] = pack(pair(tiles[0])[0])
    halo_up[0] = pack(pair(tiles[31])[1])

    spread_rows(8)

    def leaf_up(g):
        r = up_group(g, w_lb[g])
        e0[pl.ds(8 * g + 3, 8)] = e_rows(r).reshape(8, 16, 256)
        for i in range(4):
            tiles[4 * g + i] = jnp.where(
                low_half(16), r[32 * i : 32 * i + 16], r[32 * i + 16 : 32 * i + 32]
            )

    each(8, UP_UNROLL, leaf_up)

    def keep_ends(slot, nodes):
        for i in range(3):
            first, last = tiles[i // 2], tiles[(nodes - 3 + i) // 2]
            halo_down[slot + i] = pack(pair(first)[i % 2])
            halo_up[slot + i] = pack(pair(last)[(nodes - 3 + i) % 2])

    keep_ends(1, 64)

    def climb(groups, w_ref, e_ref):
        spread_rows(groups)

        def step(g):
            r = up_group(g, w_ref[g])
            parents = [r[32 * i : 32 * i + 16] + r[32 * i + 16 : 32 * i + 32] for i in range(4)]
            for i in range(2):
                tiles[2 * g + i] = jnp.where(low_half(16), parents[2 * i], parents[2 * i + 1])
            for i in range(4):
                e_ref[4 * g + 3 + i] = e_rows(parents[i])

        each(groups, UP_UNROLL, step)

    climb(8, w_t1, e1)
    keep_ends(4, 32)
    climb(4, w_t2, e2)
    keep_ends(7, 16)

    spread_rows(2)
    rooted = jnp.zeros((16, 128), F32)
    for g in range(2):
        r = up_group(g, w_tr[g])
        for n in range(8):
            rooted = rooted + r[16 * n : 16 * n + 16]
    offered = pack(dot(rooted[:, :64], lift_wide, EXACT))
    a_send[...] = offered
    a_buf[0] = offered

    pl.semaphore_wait(barrier, 2 + 7 + count - 1)

    def remote(src, dst, send, receive, device):
        return pltpu.make_async_remote_copy(
            src_ref=src, dst_ref=dst, send_sem=send, recv_sem=receive,
            device_id=(device,), device_id_type=MESH,
        )

    def a_copy(q):
        return remote(a_send, a_buf.at[q], a_ssem.at[q], a_rsem.at[q], mate(q))

    def b_copy(q):
        return remote(b_send, b_buf.at[group], b_ssem.at[q], b_rsem.at[group], far_mate(q))

    def b_arrival(q):
        origin = group_at(q, -1)
        return remote(b_send, b_buf.at[origin], b_ssem.at[q], b_rsem.at[origin], far_mate(q))

    def c_copy(q):
        return remote(c_send.at[q], c_buf.at[q], c_ssem.at[q], c_rsem.at[q], far_mate(q))

    def d_copy(q):
        return remote(d_send, d_buf.at[q], d_ssem.at[q], d_rsem.at[q], mate(q))

    def over(first, last, action):
        for q in range(first, last):
            action(q)

    over(1, 8, lambda q: a_copy(q).start())
    up_copy = remote(halo_up, from_below, halo_sems.at[0], halo_sems.at[1], above)
    down_copy = remote(halo_down, from_above, halo_sems.at[2], halo_sems.at[3], below)
    up_copy.start()
    down_copy.start()

    find_points(order_v, inverse)
    up_copy.wait_recv()
    down_copy.wait_recv()

    def fill(e_ref, nodes, width, slot):
        for i in range(width):
            lower = jnp.where(me == 0, 0.0, unpack(from_below[slot + i]))
            upper = jnp.where(me == devices - 1, 0.0, unpack(from_above[slot + i]))
            e_ref[i] = e_rows(lower)
            e_ref[nodes + width + i] = e_rows(upper)

    fill(e_ord, 64, 1, 0)
    fill(e0, 64, 3, 1)
    fill(e1, 32, 3, 4)
    fill(e2, 16, 3, 7)

    def partners(g, picks, blocks, e_ref, shift, result):
        lhs, w = [], []
        for s in range(3):
            rows = []
            for n in range(8):
                node = 8 * g + n
                rows.append(e_ref[node + shift(picks[s, node])])
            lhs.append(jnp.concatenate(rows, axis=0))
            w.append(prepare(group_of(blocks.at[s], g)))
        result[g] = pick_diagonal(times(lhs, w), 8)

    def near_shift(pick):
        return pick + 1

    def far_shift(pick):
        return pick + (pick >> 1) * 3

    def near_part(first):
        each(
            4,
            NEAR_UNROLL,
            lambda g: partners(g + first, near_pick, near_v, e_ord, near_shift, near_f),
        )

    loads["near"].wait()
    near_part(0)

    over(1, 8, lambda q: a_copy(q).wait_recv())

    def total_of(buffer, slots):
        result = buffer[0]
        for q in range(1, slots):
            result = result + buffer[q]
        return result

    summed = total_of(a_buf, 8)
    b_send[...] = summed
    b_buf[group] = summed
    over(1, count, lambda q: b_copy(q).start())

    near_part(4)
    loads["tb"].wait()
    tb_v[0:4, :] = tb4_v[...]
    tb_v[4:8, :] = jnp.zeros((4, 4096), F32)
    w_top = prepare(tb_v[...])

    over(1, count, lambda q: b_arrival(q).wait_recv())

    picked = []
    for b in range(4):
        picked.append(e_rows(unpack(b_buf[top_source[b]])))
    coupled = pick_diagonal(times([jnp.concatenate(picked, axis=0)], [w_top]), 4)
    head, rest = split(coupled)
    moved = dot(jnp.concatenate([head, rest], axis=0), to_n[:, 0:256])
    moved = moved[0:16] + moved[16:32]
    packed = []
    for i in range(2):
        packed += [pack(block) for block in pair(moved[:, 128 * i : 128 * i + 128])]
    for q in range(count):
        target = group_at(q)
        part = jnp.zeros((8, 128), F32)
        for b in range(4):
            part = part + jnp.where(jnp.full((8, 128), top_target[b]) == target, packed[b], 0.0)
        if q == 0:
            c_buf[0] = part
        else:
            c_send[q] = part
    over(1, count, lambda q: c_copy(q).start())

    loads["fa"].wait()
    each(8, NEAR_UNROLL, lambda g: partners(g, pick_a, fa_v, e0, far_shift, far_a))

    over(1, count, lambda q: c_copy(q).wait_recv())
    summed = total_of(c_buf, count)
    d_send[...] = summed
    d_buf[0] = summed
    over(1, 8, lambda q: d_copy(q).start())

    loads["fb"].wait()
    each(4, NEAR_UNROLL, lambda g: partners(g, pick_b, fb_v, e1, far_shift, far_b))
    loads["fc"].wait()
    each(2, NEAR_UNROLL, lambda g: partners(g, pick_c, fc_v, e2, far_shift, far_c))

    over(1, 8, lambda q: d_copy(q).wait_recv())
    falling = unpack(total_of(d_buf, 8))
    root_down = dot_nt(falling[:, :64], lift_tall, EXACT)

    def to_e(values, groups):
        head, rest = split(values)
        rows = groups * 16
        moved = dot(jnp.concatenate([head, rest], axis=0), to_n[...])
        for g in range(groups):
            for i in range(4):
                at = slice(128 * i, 128 * i + 128)
                heads = pair(moved[16 * g : 16 * g + 16, at])
                rests = pair(moved[rows + 16 * g : rows + 16 * g + 16, at])
                for k in range(2):
                    node = 8 * g + 2 * i + k
                    e_down[node] = jnp.concatenate(
                        [heads[k].astype(BF16), rests[k].astype(BF16)], axis=1
                    )

    def parents_of(g):
        rows = []
        for n in range(4):
            block = e_down[4 * g + n]
            rows += [block, block]
        return jnp.concatenate(rows, axis=0)

    root_e = e_rows(root_down)
    values = [far_c[g] + times([root_e], [w_tr[g]]) for g in range(2)]
    to_e(jnp.concatenate(values, axis=0), 2)

    def descend(groups, w_ref, far):
        def step(g):
            far[g] = far[g] + pick_diagonal(times([parents_of(g)], [w_ref[g]]), 8)

        each(groups, UP_UNROLL, step)
        to_e(jnp.concatenate([far[g] for g in range(groups)], axis=0), groups)

    descend(4, w_t2, far_b)
    descend(8, w_t1, far_a)

    def leaf_down(g):
        lhs = e_down[pl.ds(8 * g, 8)].reshape(128, 256)
        value = near_f[g] + pick_diagonal(times([lhs], [w_lb[g]]), 8)
        for i in range(4):
            vals[4 * g + i] = value[:, 128 * i : 128 * i + 128]

    each(8, UP_UNROLL, leaf_down)

    up_copy.wait_send()
    down_copy.wait_send()
    over(1, 8, lambda q: a_copy(q).wait_send())
    over(1, count, lambda q: b_copy(q).wait_send())
    over(1, count, lambda q: c_copy(q).wait_send())
    over(1, 8, lambda q: d_copy(q).wait_send())


def restore(vals, inverse, out):
    table = table_of([vals[t] for t in range(32)])
    for j in range(8):
        rows = [inverse[4 * j + i : 4 * j + i + 1, :] for i in range(4)]
        lanes = [inverse[4 * j + i + 32 : 4 * j + i + 33, :] for i in range(4)]
        out[:, 512 * j : 512 * j + 512] = lookup(
            table, jnp.concatenate(rows, axis=1), jnp.concatenate(lanes, axis=1)
        )


def body(devices, *args):
    smem, hbm = pl.BlockSpec(memory_space=pltpu.SMEM), pl.BlockSpec(memory_space=pl.ANY)
    vm, whole = pltpu.VMEM, pl.BlockSpec(memory_space=pltpu.VMEM)
    small = (3, 8, 10, 12, 15, 16)
    count = devices // 8
    big = [0, 1, 2, 4, 5, 6, 7, 9, 11, 13, 14, 17]
    dma = pltpu.SemaphoreType.DMA
    scratch = [vm(args[i].shape, args[i].dtype) for i in big]
    scratch += [
        vm((8, 4096), F32),
        vm((8, 512, 128), BF16),
        vm((8, 512, 128), BF16),
        vm((4, 512, 128), BF16),
        vm((2, 512, 128), BF16),
        vm((512, 512), BF16),
        vm((512, 512), BF16),
        vm((128, 512), BF16),
        vm((2, 128, 512), BF16),
        vm((512, 256), BF16),
        vm((32, 16, 128), F32),
        vm((66, 16, 256), BF16),
        vm((70, 16, 256), BF16),
        vm((38, 16, 256), BF16),
        vm((22, 16, 256), BF16),
        vm((64, 16, 256), BF16),
        vm((8, 16, 512), F32),
        vm((8, 16, 512), F32),
        vm((4, 16, 512), F32),
        vm((2, 16, 512), F32),
        vm((3, 32, 128), F32),
        vm((10, 8, 128), F32),
        vm((10, 8, 128), F32),
        vm((10, 8, 128), F32),
        vm((10, 8, 128), F32),
        vm((8, 128), F32),
        vm((8, 8, 128), F32),
        vm((8, 128), F32),
        vm((count, 8, 128), F32),
        vm((count, 8, 128), F32),
        vm((count, 8, 128), F32),
        vm((8, 128), F32),
        vm((8, 8, 128), F32),
        dma((12,)),
        dma((4,)),
        dma((8,)),
        dma((8,)),
        dma((count,)),
        dma((count,)),
        dma((count,)),
        dma((count,)),
        dma((8,)),
        dma((8,)),
    ]
    vals, inverse = pl.pallas_call(
        functools.partial(kernel, devices),
        out_shape=(
            jax.ShapeDtypeStruct((32, 16, 128), F32),
            jax.ShapeDtypeStruct((64, 128), I32),
        ),
        in_specs=[smem if i in small else hbm for i in range(18)],
        out_specs=(whole, whole),
        scratch_shapes=scratch,
        compiler_params=pltpu.CompilerParams(
            collective_id=0, has_side_effects=True, vmem_limit_bytes=60 * 1024 * 1024
        ),
    )(*args)
    return pl.pallas_call(
        restore,
        out_shape=jax.ShapeDtypeStruct((16, 4096), F32),
        in_specs=[whole] * 2,
        out_specs=whole,
        compiler_params=pltpu.CompilerParams(vmem_limit_bytes=60 * 1024 * 1024),
    )(vals, inverse)


def solution(mesh):
    split_rows, split_columns = P("leaf", None), P(None, "leaf")
    split_middle = P(None, "leaf", None)
    in_specs = (
        split_columns,
        split_rows,
        split_rows,
        split_columns,
        split_middle,
        split_rows,
        split_rows,
        split_rows,
        split_columns,
        split_middle,
        split_columns,
        split_middle,
        split_columns,
        split_middle,
        split_middle,
        P("leaf"),
        P("leaf"),
        split_rows,
    )
    return jax.shard_map(
        functools.partial(body, mesh.shape["leaf"]),
        mesh=mesh,
        in_specs=in_specs,
        out_specs=split_columns,
        check_vma=False,
    )
```

```python
import functools

import jax
import jax.numpy as jnp
from jax import lax
from jax.experimental import pallas as pl
from jax.experimental.pallas import tpu as pltpu
from jax.sharding import PartitionSpec as P

F32, BF16, I32 = jnp.float32, jnp.bfloat16, jnp.int32
MESH = pl.DeviceIdType.MESH
EXACT = lax.Precision.HIGHEST
NEAR_UNROLL = 2
UP_UNROLL = 8
DOWN_UNROLL = 4
Z_UNROLL = 1


def iota(shape, dim):
    return lax.broadcasted_iota(I32, shape, dim)


def dot(a, b, precision=None):
    return lax.dot_general(
        a, b, (((1,), (0,)), ((), ())), precision=precision, preferred_element_type=F32
    )


def dot_nt(a, b, precision=None):
    return lax.dot_general(
        a, b, (((1,), (1,)), ((), ())), precision=precision, preferred_element_type=F32
    )


def split(x):
    head = x.astype(BF16)
    return head, (x - head.astype(F32)).astype(BF16)


def low_half(rows):
    return iota((rows, 128), 1) < 64


def swap(x):
    return pltpu.roll(x, 64, 1)


def prepare(block):
    a = jnp.concatenate([block[:, 128 * c : 128 * c + 128] for c in range(32)], axis=0)
    rest = a - a.astype(BF16).astype(F32)
    low = low_half(256)
    first = jnp.where(low, a, rest)
    second = swap(jnp.where(low, rest, a))
    top = jnp.where(low, first, second)
    bottom = jnp.where(low, second, first)
    return jnp.concatenate([top, bottom], axis=0).astype(BF16)


def pack(block):
    return jnp.where(low_half(8), block[0:8], block[8:16])


def unpack(packed):
    low, other = low_half(8), swap(packed)
    return jnp.concatenate(
        [jnp.where(low, packed, other), jnp.where(low, other, packed)], axis=0
    )


def pair(tile):
    low, other = low_half(tile.shape[0]), swap(tile)
    return jnp.where(low, tile, other), jnp.where(low, other, tile)


def e_rows(block):
    head, rest = split(block)
    return jnp.concatenate([head, rest], axis=1)


def pick_diagonal(wide, nodes, rows=16):
    lane_node = iota((rows, 512), 1) & 7
    result = wide[0:rows]
    for n in range(1, nodes):
        result = jnp.where(lane_node == n, wide[rows * n : rows * n + rows], result)
    return result


def table_of(tiles):
    head, rest = split(jnp.concatenate(tiles, axis=0))
    return jnp.concatenate([head, rest], axis=1)


def lookup(table, tile_index, lane_index):
    width = lane_index.shape[1]
    hot = jnp.where(iota((128, width), 0) == lane_index, 1.0, 0.0).astype(BF16)
    found = dot(table, jnp.concatenate([hot, hot], axis=0))
    tile_index = jnp.broadcast_to(tile_index, (16, width))
    result = found[0:16]
    for s in range(1, 32):
        result = jnp.where(tile_index == s, found[16 * s : 16 * s + 16], result)
    return result


def find_points(order, inverse):
    def step(j, total):
        row = order[:, pl.ds(pl.multiple_of(j * 512, 512), 512)]
        lane = iota((1, 512), 1)
        n, p = lane >> 6, lane & 63
        parity, c = p & 1, p >> 1
        tile = (j * 4 + parity * 2 + (c >> 4)).astype(F32)
        place = ((c & 15) * 8 + n).astype(F32)
        chosen = iota((32, 512), 0) == (row >> 7)
        rows = jnp.concatenate(
            [jnp.where(chosen, tile, 0.0), jnp.where(chosen, place, 0.0)], axis=0
        ).astype(BF16)
        columns = jnp.where(iota((128, 512), 0) == (row & 127), 1.0, 0.0).astype(BF16)
        return total + dot_nt(rows, columns)

    inverse[...] = lax.fori_loop(0, 8, step, jnp.zeros((64, 128), F32), unroll=2).astype(I32)


def times(lhs_terms, w_terms):
    lhs = jnp.concatenate(lhs_terms, axis=1)
    w = jnp.concatenate([w for term in w_terms for w in (term, term)], axis=1)
    return dot_nt(lhs, w)


def kernel(
    devices,
    rhs_h, order_h, lb_h, near_pick, near_h, t1_h, t2_h, tr_h,
    pick_a, fa_h, pick_b, fb_h, pick_c, fc_h, tt_h, top_source, top_target, tb_h,
    vals, inverse,
    rhs_v, order_v, lb_v, near_v, t1_v, t2_v, tr_v, fa_v, fb_v, fc_v, tt_v, tb4_v,
    tb_v, w_lb, w_t1, w_t2, w_tr, to_d, to_n, diagonal, dmat, table, tiles,
    e_ord, e0, e1, e2, e_down, z_d, z_e, z_w, lift_rows, near_f, far_a, far_b, far_c,
    t_rows, halo_up, halo_down, from_below, from_above,
    a_send, a_buf, b_send, b_buf, c_send, c_buf, d_send, d_buf,
    load_sem, halo_sems, a_ssem, a_rsem, b_ssem, b_rsem, c_ssem, c_rsem, d_ssem, d_rsem,
):
    me = lax.axis_index("leaf")
    count = devices // 8
    inside, group = me & 7, me >> 3
    base = me - inside
    above, below = (me + 1) & (devices - 1), (me + devices - 1) & (devices - 1)
    deep = min(8, count)
    wide = count // deep
    line, depth = group // deep, group & (deep - 1)

    def hops(offset):
        dx, dz = offset
        return min(dx, wide - dx) + min(dz, deep - dz)

    offsets = sorted(((dx, dz) for dx in range(wide) for dz in range(deep)), key=hops)[::-1]
    offsets = [(0, 0)] + offsets[:-1]

    def group_at(q, sign=1):
        dx, dz = offsets[q]
        dx, dz = (dx, dz) if sign > 0 else (wide - dx, deep - dz)
        return ((line + dx) & (wide - 1)) * deep + ((depth + dz) & (deep - 1))

    def mate(q):
        return base + ((inside + q) & 7)

    def far_mate(q):
        return group_at(q) * 8 + inside

    loads = {}

    def load(**pairs):
        for name, (src, dst) in pairs.items():
            loads[name] = pltpu.make_async_copy(src, dst, load_sem.at[len(loads)])
            loads[name].start()

    load(order=(order_h, order_v), rhs=(rhs_h, rhs_v), lb=(lb_h, lb_v), t1=(t1_h, t1_v))
    load(t2=(t2_h, t2_v), tr=(tr_h, tr_v), tt=(tt_h, tt_v))

    barrier = pltpu.get_barrier_semaphore()

    def greet(device):
        pl.semaphore_signal(barrier, inc=1, device_id=(device,), device_id_type=MESH)

    greet(above)
    greet(below)

    @pl.loop(1, 8)
    def _(q):
        greet(mate(q))

    for q in range(1, count):
        greet(far_mate(q))

    n_lane, d_lane = iota((512, 512), 0), iota((512, 512), 1)
    wanted = (d_lane & 7) * 64 + ((d_lane >> 3) & 31) * 2 + (d_lane >> 8)
    to_d[...] = jnp.where(n_lane == wanted, 1.0, 0.0).astype(BF16)
    wanted = (n_lane & 7) * 64 + ((n_lane >> 3) & 31) * 2 + (n_lane >> 8)
    to_n[...] = jnp.where(d_lane == wanted, 1.0, 0.0).astype(BF16)
    diagonal[...] = jnp.where(
        (iota((128, 512), 1) & 7) == (iota((128, 512), 0) >> 4), 1.0, 0.0
    ).astype(BF16)

    loads["rhs"].wait()
    table[...] = table_of([rhs_v[:, 128 * t : 128 * t + 128] for t in range(32)])
    loads["order"].wait()

    def group_of(ref, g):
        return ref[pl.ds(pl.multiple_of(g * 8, 8), 8), :]

    split_next = [
        (name, ref, w, g)
        for name, ref, w, groups in (
            ("lb", lb_v, w_lb, 8), ("t1", t1_v, w_t1, 8), ("t2", t2_v, w_t2, 4), ("tr", tr_v, w_tr, 2)
        )
        for g in range(groups)
    ]
    for j in range(8):
        row = order_v[:, 512 * j : 512 * j + 512]
        found = lookup(table[...], row >> 7, row & 127)
        for i in range(4):
            tile = found[:, 128 * i : 128 * i + 128]
            tiles[4 * j + i] = tile
            for k, block in enumerate(pair(tile)):
                e_ord[8 * j + 2 * i + k + 1] = e_rows(block)
        for _ in range(min(j + 1, 3)):
            name, ref, w, g = split_next.pop(0)
            if g == 0:
                loads[name].wait()
            w[g] = prepare(group_of(ref, g))
    while split_next:
        name, ref, w, g = split_next.pop(0)
        w[g] = prepare(group_of(ref, g))
    load(near=(near_h, near_v), fa=(fa_h, fa_v), fb=(fb_h, fb_v), fc=(fc_h, fc_v), tb=(tb_h, tb4_v))

    loads["tt"].wait()
    for j in range(3):
        for c in range(32):
            t_rows[j, c : c + 1, :] = tt_v[j, :, 128 * c : 128 * c + 128]
    sort = jnp.where(
        iota((64, 64), 0) == (iota((64, 64), 1) & 31) * 2 + (iota((64, 64), 1) >> 5), 1.0, 0.0
    ).astype(F32)

    def top_matrix(j):
        rows = t_rows[j]
        return dot(sort, jnp.concatenate([rows[:, :64], rows[:, 64:]], axis=0), EXACT)

    lift = dot(top_matrix(0), dot(top_matrix(1), top_matrix(2), EXACT), EXACT)
    lift_wide = jnp.concatenate([lift, lift], axis=1)
    lift_rows[...] = lift

    def spread_rows(groups):
        x = jnp.concatenate(
            [
                jnp.concatenate([tiles[4 * g + i] for i in range(4)], axis=1)
                for g in range(groups)
            ],
            axis=0,
        )
        head, rest = split(x)
        rows = groups * 16
        moved = dot(jnp.concatenate([head, rest], axis=0), to_d[...]).astype(BF16)
        dmat[0, 0:rows, :] = moved[0:rows]
        dmat[1, 0:rows, :] = moved[rows:]

    def up_group(g, w):
        at = pl.ds(pl.multiple_of(g * 16, 16), 16)
        mask = diagonal[...]
        lhs = jnp.concatenate(
            [
                jnp.concatenate([dmat[0, at, :]] * 8, axis=0) * mask,
                jnp.concatenate([dmat[1, at, :]] * 8, axis=0) * mask,
            ],
            axis=0,
        )
        product = dot(lhs, w)
        both = product[0:128] + product[128:256]
        return both + swap(both)

    def each(groups, unroll, step):
        def body(g, carry):
            step(g)
            return carry

        lax.fori_loop(0, groups, body, 0, unroll=min(unroll, groups))

    halo_down[0] = pack(pair(tiles[0])[0])
    halo_up[0] = pack(pair(tiles[31])[1])

    spread_rows(8)

    def leaf_up(g):
        r = up_group(g, w_lb[g])
        e0[pl.ds(8 * g + 3, 8)] = e_rows(r).reshape(8, 16, 256)
        for i in range(4):
            tiles[4 * g + i] = jnp.where(
                low_half(16), r[32 * i : 32 * i + 16], r[32 * i + 16 : 32 * i + 32]
            )

    each(8, UP_UNROLL, leaf_up)

    def keep_ends(slot, nodes):
        for i in range(3):
            first, last = tiles[i // 2], tiles[(nodes - 3 + i) // 2]
            halo_down[slot + i] = pack(pair(first)[i % 2])
            halo_up[slot + i] = pack(pair(last)[(nodes - 3 + i) % 2])

    keep_ends(1, 64)

    def climb(groups, w_ref, e_ref):
        spread_rows(groups)

        def step(g):
            r = up_group(g, w_ref[g])
            parents = [r[32 * i : 32 * i + 16] + r[32 * i + 16 : 32 * i + 32] for i in range(4)]
            for i in range(2):
                tiles[2 * g + i] = jnp.where(low_half(16), parents[2 * i], parents[2 * i + 1])
            for i in range(4):
                e_ref[4 * g + 3 + i] = e_rows(parents[i])

        each(groups, UP_UNROLL, step)

    climb(8, w_t1, e1)
    keep_ends(4, 32)
    climb(4, w_t2, e2)
    keep_ends(7, 16)

    spread_rows(2)
    rooted = jnp.zeros((16, 128), F32)
    for g in range(2):
        r = up_group(g, w_tr[g])
        for n in range(8):
            rooted = rooted + r[16 * n : 16 * n + 16]
    offered = pack(dot(rooted[:, :64], lift_wide, EXACT))
    a_send[...] = offered
    a_buf[0] = offered

    pl.semaphore_wait(barrier, 2 + 7 + count - 1)

    def remote(src, dst, send, receive, device):
        return pltpu.make_async_remote_copy(
            src_ref=src, dst_ref=dst, send_sem=send, recv_sem=receive,
            device_id=(device,), device_id_type=MESH,
        )

    def a_copy(q):
        return remote(a_send, a_buf.at[q], a_ssem.at[q], a_rsem.at[q], mate(q))

    def b_copy(q):
        return remote(b_send, b_buf.at[group], b_ssem.at[q], b_rsem.at[group], far_mate(q))

    def b_arrival(q):
        origin = group_at(q, -1)
        return remote(b_send, b_buf.at[origin], b_ssem.at[q], b_rsem.at[origin], far_mate(q))

    def c_copy(q):
        return remote(c_send.at[q], c_buf.at[q], c_ssem.at[q], c_rsem.at[q], far_mate(q))

    def d_copy(q):
        return remote(d_send, d_buf.at[q], d_ssem.at[q], d_rsem.at[q], mate(q))

    def over(first, last, action):
        for q in range(first, last):
            action(q)

    over(1, 8, lambda q: a_copy(q).start())
    up_copy = remote(halo_up, from_below, halo_sems.at[0], halo_sems.at[1], above)
    down_copy = remote(halo_down, from_above, halo_sems.at[2], halo_sems.at[3], below)
    up_copy.start()
    down_copy.start()

    find_points(order_v, inverse)
    up_copy.wait_recv()
    down_copy.wait_recv()

    def fill(e_ref, nodes, width, slot):
        for i in range(width):
            lower = jnp.where(me == 0, 0.0, unpack(from_below[slot + i]))
            upper = jnp.where(me == devices - 1, 0.0, unpack(from_above[slot + i]))
            e_ref[i] = e_rows(lower)
            e_ref[nodes + width + i] = e_rows(upper)

    fill(e_ord, 64, 1, 0)
    fill(e0, 64, 3, 1)
    fill(e1, 32, 3, 4)
    fill(e2, 16, 3, 7)

    def partners(g, picks, blocks, e_ref, shift, result):
        lhs, w = [], []
        for s in range(3):
            rows = []
            for n in range(8):
                node = 8 * g + n
                rows.append(e_ref[node + shift(picks[s, node])])
            lhs.append(jnp.concatenate(rows, axis=0))
            w.append(prepare(group_of(blocks.at[s], g)))
        result[g] = pick_diagonal(times(lhs, w), 8)

    def near_shift(pick):
        return pick + 1

    def far_shift(pick):
        return pick + (pick >> 1) * 3

    def near_part(first):
        each(
            4,
            NEAR_UNROLL,
            lambda g: partners(g + first, near_pick, near_v, e_ord, near_shift, near_f),
        )

    def parents_of(e_ref, g):
        rows = []
        for n in range(4):
            block = e_ref[4 * g + n]
            rows += [block, block]
        return jnp.concatenate(rows, axis=0)

    def to_e(source, e_ref, groups, rows, unroll):
        def step(g):
            head, rest = split(source[g])
            moved = dot(jnp.concatenate([head, rest], axis=0), to_n[...])
            for i in range(4):
                at = slice(128 * i, 128 * i + 128)
                heads, rests = pair(moved[0:rows, at]), pair(moved[rows:, at])
                for k in range(2):
                    e_ref[8 * g + 2 * i + k] = jnp.concatenate(
                        [heads[k].astype(BF16), rests[k].astype(BF16)], axis=1
                    )

        each(groups, unroll, step)

    def compose_two():
        lift_t = dot_nt(
            jnp.where(iota((64, 64), 0) == iota((64, 64), 1), 1.0, 0.0).astype(F32),
            lift_rows[...],
            EXACT,
        )
        start = e_rows(jnp.concatenate([lift_t, lift_t], axis=1))
        for g in range(2):
            z_d[g] = times([start], [w_tr[g]])
        to_e(z_d, z_e, 2, 64, 2)

    def compose(groups, w_ref):
        def step(g):
            z_d[g] = pick_diagonal(times([parents_of(z_e, g)], [w_ref[g]]), 8, 64)

        each(groups, Z_UNROLL, step)
        to_e(z_d, z_e, groups, 64, Z_UNROLL)

    def compose_leaves():
        def step(g):
            lhs = z_e[pl.ds(8 * g, 8)].reshape(512, 256)
            head, rest = split(pick_diagonal(times([lhs], [w_lb[g]]), 8, 64))
            z_w[g] = jnp.concatenate([head, rest, head, rest], axis=0)

        each(8, Z_UNROLL, step)

    def descend(groups, w_ref, far):
        def step(g):
            far[g] = far[g] + pick_diagonal(times([parents_of(e_down, g)], [w_ref[g]]), 8)

        each(groups, DOWN_UNROLL, step)
        to_e(far, e_down, groups, 16, DOWN_UNROLL)

    compose_two()
    compose(4, w_t2)
    loads["fc"].wait()
    each(2, NEAR_UNROLL, lambda g: partners(g, pick_c, fc_v, e2, far_shift, far_c))
    loads["fb"].wait()
    each(4, NEAR_UNROLL, lambda g: partners(g, pick_b, fb_v, e1, far_shift, far_b))

    over(1, 8, lambda q: a_copy(q).wait_recv())

    def total_of(buffer, slots):
        result = buffer[0]
        for q in range(1, slots):
            result = result + buffer[q]
        return result

    summed = total_of(a_buf, 8)
    b_send[...] = summed
    b_buf[group] = summed
    over(1, count, lambda q: b_copy(q).start())

    compose(8, w_t1)
    compose_leaves()
    loads["near"].wait()
    near_part(0)
    loads["tb"].wait()
    tb_v[0:4, :] = tb4_v[...]
    tb_v[4:8, :] = jnp.zeros((4, 4096), F32)
    w_top = prepare(tb_v[...])

    over(1, count, lambda q: b_arrival(q).wait_recv())

    picked = []
    for b in range(4):
        picked.append(e_rows(unpack(b_buf[top_source[b]])))
    coupled = pick_diagonal(times([jnp.concatenate(picked, axis=0)], [w_top]), 4)
    head, rest = split(coupled)
    moved = dot(jnp.concatenate([head, rest], axis=0), to_n[:, 0:256])
    moved = moved[0:16] + moved[16:32]
    packed = []
    for i in range(2):
        packed += [pack(block) for block in pair(moved[:, 128 * i : 128 * i + 128])]
    for q in range(count):
        target = group_at(q)
        part = jnp.zeros((8, 128), F32)
        for b in range(4):
            part = part + jnp.where(jnp.full((8, 128), top_target[b]) == target, packed[b], 0.0)
        if q == 0:
            c_buf[0] = part
        else:
            c_send[q] = part
    over(1, count, lambda q: c_copy(q).start())

    near_part(4)
    loads["fa"].wait()
    each(8, NEAR_UNROLL, lambda g: partners(g, pick_a, fa_v, e0, far_shift, far_a))

    over(1, count, lambda q: c_copy(q).wait_recv())
    summed = total_of(c_buf, count)
    d_send[...] = summed
    d_buf[0] = summed
    over(1, 8, lambda q: d_copy(q).start())

    to_e(far_c, e_down, 2, 16, 2)
    descend(4, w_t2, far_b)
    descend(8, w_t1, far_a)

    def leaf_down(g):
        lhs = e_down[pl.ds(8 * g, 8)].reshape(128, 256)
        near_f[g] = near_f[g] + pick_diagonal(times([lhs], [w_lb[g]]), 8)

    each(8, DOWN_UNROLL, leaf_down)

    over(1, 8, lambda q: d_copy(q).wait_recv())
    falling = e_rows(unpack(total_of(d_buf, 8)))

    for g in range(8):
        value = near_f[g] + dot(falling, z_w[g])
        for i in range(4):
            vals[4 * g + i] = value[:, 128 * i : 128 * i + 128]

    up_copy.wait_send()
    down_copy.wait_send()
    over(1, 8, lambda q: a_copy(q).wait_send())
    over(1, count, lambda q: b_copy(q).wait_send())
    over(1, count, lambda q: c_copy(q).wait_send())
    over(1, 8, lambda q: d_copy(q).wait_send())


def restore(vals, inverse, out):
    table = table_of([vals[t] for t in range(32)])
    for j in range(8):
        rows = [inverse[4 * j + i : 4 * j + i + 1, :] for i in range(4)]
        lanes = [inverse[4 * j + i + 32 : 4 * j + i + 33, :] for i in range(4)]
        out[:, 512 * j : 512 * j + 512] = lookup(
            table, jnp.concatenate(rows, axis=1), jnp.concatenate(lanes, axis=1)
        )


def body(devices, *args):
    smem, hbm = pl.BlockSpec(memory_space=pltpu.SMEM), pl.BlockSpec(memory_space=pl.ANY)
    vm, whole = pltpu.VMEM, pl.BlockSpec(memory_space=pltpu.VMEM)
    small = (3, 8, 10, 12, 15, 16)
    count = devices // 8
    big = [0, 1, 2, 4, 5, 6, 7, 9, 11, 13, 14, 17]
    dma = pltpu.SemaphoreType.DMA
    scratch = [vm(args[i].shape, args[i].dtype) for i in big]
    scratch += [
        vm((8, 4096), F32),
        vm((8, 512, 128), BF16),
        vm((8, 512, 128), BF16),
        vm((4, 512, 128), BF16),
        vm((2, 512, 128), BF16),
        vm((512, 512), BF16),
        vm((512, 512), BF16),
        vm((128, 512), BF16),
        vm((2, 128, 512), BF16),
        vm((512, 256), BF16),
        vm((32, 16, 128), F32),
        vm((66, 16, 256), BF16),
        vm((70, 16, 256), BF16),
        vm((38, 16, 256), BF16),
        vm((22, 16, 256), BF16),
        vm((64, 16, 256), BF16),
        vm((8, 64, 512), F32),
        vm((64, 64, 256), BF16),
        vm((8, 256, 512), BF16),
        vm((64, 64), F32),
        vm((8, 16, 512), F32),
        vm((8, 16, 512), F32),
        vm((4, 16, 512), F32),
        vm((2, 16, 512), F32),
        vm((3, 32, 128), F32),
        vm((10, 8, 128), F32),
        vm((10, 8, 128), F32),
        vm((10, 8, 128), F32),
        vm((10, 8, 128), F32),
        vm((8, 128), F32),
        vm((8, 8, 128), F32),
        vm((8, 128), F32),
        vm((count, 8, 128), F32),
        vm((count, 8, 128), F32),
        vm((count, 8, 128), F32),
        vm((8, 128), F32),
        vm((8, 8, 128), F32),
        dma((12,)),
        dma((4,)),
        dma((8,)),
        dma((8,)),
        dma((count,)),
        dma((count,)),
        dma((count,)),
        dma((count,)),
        dma((8,)),
        dma((8,)),
    ]
    vals, inverse = pl.pallas_call(
        functools.partial(kernel, devices),
        out_shape=(
            jax.ShapeDtypeStruct((32, 16, 128), F32),
            jax.ShapeDtypeStruct((64, 128), I32),
        ),
        in_specs=[smem if i in small else hbm for i in range(18)],
        out_specs=(whole, whole),
        scratch_shapes=scratch,
        compiler_params=pltpu.CompilerParams(
            collective_id=0, has_side_effects=True, vmem_limit_bytes=60 * 1024 * 1024
        ),
    )(*args)
    return pl.pallas_call(
        restore,
        out_shape=jax.ShapeDtypeStruct((16, 4096), F32),
        in_specs=[whole] * 2,
        out_specs=whole,
        compiler_params=pltpu.CompilerParams(vmem_limit_bytes=60 * 1024 * 1024),
    )(vals, inverse)


def solution(mesh):
    split_rows, split_columns = P("leaf", None), P(None, "leaf")
    split_middle = P(None, "leaf", None)
    in_specs = (
        split_columns,
        split_rows,
        split_rows,
        split_columns,
        split_middle,
        split_rows,
        split_rows,
        split_rows,
        split_columns,
        split_middle,
        split_columns,
        split_middle,
        split_columns,
        split_middle,
        split_middle,
        P("leaf"),
        P("leaf"),
        split_rows,
    )
    return jax.shard_map(
        functools.partial(body, mesh.shape["leaf"]),
        mesh=mesh,
        in_specs=in_specs,
        out_specs=split_columns,
        check_vma=False,
    )
```

```python
import functools

import jax
import jax.numpy as jnp
from jax import lax
from jax.experimental import pallas as pl
from jax.experimental.pallas import tpu as pltpu
from jax.sharding import PartitionSpec as P

F32, BF16, I32 = jnp.float32, jnp.bfloat16, jnp.int32
MESH = pl.DeviceIdType.MESH
EXACT = lax.Precision.HIGHEST
NEAR_UNROLL = 2
UP_UNROLL = 8


def iota(shape, dim):
    return lax.broadcasted_iota(I32, shape, dim)


def dot(a, b, precision=None):
    return lax.dot_general(
        a, b, (((1,), (0,)), ((), ())), precision=precision, preferred_element_type=F32
    )


def dot_nt(a, b, precision=None):
    return lax.dot_general(
        a, b, (((1,), (1,)), ((), ())), precision=precision, preferred_element_type=F32
    )


def split(x):
    head = x.astype(BF16)
    return head, (x - head.astype(F32)).astype(BF16)


def low_half(rows):
    return iota((rows, 128), 1) < 64


def swap(x):
    return pltpu.roll(x, 64, 1)


def prepare(ref, g, half):
    start = g * 256 + 4 * half
    return split_rows([ref[pl.ds(start + n, 32, stride=8), :] for n in range(4)])


def split_rows(matrices):
    a = jnp.concatenate(matrices, axis=0)
    rest = a - a.astype(BF16).astype(F32)
    low = low_half(128)
    first = jnp.where(low, a, rest)
    second = swap(jnp.where(low, rest, a))
    top = jnp.where(low, first, second)
    bottom = jnp.where(low, second, first)
    return jnp.concatenate([top, bottom], axis=0).astype(BF16)


def pack(block):
    return jnp.where(low_half(8), block[0:8], block[8:16])


def unpack(packed):
    low, other = low_half(8), swap(packed)
    return jnp.concatenate(
        [jnp.where(low, packed, other), jnp.where(low, other, packed)], axis=0
    )


def pair(tile):
    low, other = low_half(16), swap(tile)
    return jnp.where(low, tile, other), jnp.where(low, other, tile)


def e_rows(block):
    head, rest = split(block)
    return jnp.concatenate([head, rest], axis=1)


def pick_diagonal(wide):
    lane_node = (iota((16, 256), 1) >> 5) & 3
    result = wide[0:16]
    for n in range(1, 4):
        result = jnp.where(lane_node == n, wide[16 * n : 16 * n + 16], result)
    return result


def table_of(tiles):
    head, rest = split(jnp.concatenate(tiles, axis=0))
    return jnp.concatenate([head, rest], axis=1)


def lookup(table, tile_index, lane_index):
    width = lane_index.shape[1]
    hot = jnp.where(iota((128, width), 0) == lane_index, 1.0, 0.0).astype(BF16)
    found = dot(table, jnp.concatenate([hot, hot], axis=0))
    tile_index = jnp.broadcast_to(tile_index, (16, width))
    result = found[0:16]
    for s in range(1, 32):
        result = jnp.where(tile_index == s, found[16 * s : 16 * s + 16], result)
    return result


def find_points(order, inverse):
    def step(j, total):
        row = order[:, pl.ds(pl.multiple_of(j * 512, 512), 512)]
        lane = iota((1, 512), 1)
        n, p = lane >> 6, lane & 63
        parity, c = p & 1, p >> 1
        tile = (j * 4 + (n >> 2) * 2 + parity).astype(F32)
        place = ((n & 3) * 32 + c).astype(F32)
        chosen = iota((32, 512), 0) == (row >> 7)
        rows = jnp.concatenate(
            [jnp.where(chosen, tile, 0.0), jnp.where(chosen, place, 0.0)], axis=0
        ).astype(BF16)
        columns = jnp.where(iota((128, 512), 0) == (row & 127), 1.0, 0.0).astype(BF16)
        return total + dot_nt(rows, columns)

    inverse[...] = lax.fori_loop(0, 8, step, jnp.zeros((64, 128), F32), unroll=2).astype(I32)


def times(lhs_terms, w_terms):
    rows = lhs_terms[0].shape[0]
    heads = jnp.concatenate([lhs[:, :128] for lhs in lhs_terms], axis=1)
    rests = jnp.concatenate([lhs[:, 128:] for lhs in lhs_terms], axis=1)
    both = dot_nt(jnp.concatenate([heads, rests], axis=0), jnp.concatenate(w_terms, axis=1))
    return both[:rows] + both[rows:]


def kernel(
    devices,
    rhs_h, order_h, lb_h, near_pick, near_h, t1_h, t2_h, tr_h,
    pick_a, fa_h, pick_b, fb_h, pick_c, fc_h, tt_h, top_source, top_target, tb_h,
    vals, inverse,
    rhs_v, order_v, lb_v, near_v, t1_v, t2_v, tr_v, fa_v, fb_v, fc_v, tt_v, tb_v,
    w_lb, w_t1, w_t2, w_tr, to_d, to_n, diagonal, dmat, table, tiles,
    e_ord, e0, e1, e2, e_down, near_f, far_a, far_b, far_c,
    halo_up, halo_down, from_below, from_above,
    a_send, a_buf, b_send, b_buf, c_send, c_buf, d_send, d_buf,
    load_sem, halo_sems, a_ssem, a_rsem, b_ssem, b_rsem, c_ssem, c_rsem, d_ssem, d_rsem,
):
    me = lax.axis_index("leaf")
    count = devices // 8
    inside, group = me & 7, me >> 3
    base = me - inside
    above, below = (me + 1) & (devices - 1), (me + devices - 1) & (devices - 1)
    deep = min(8, count)
    wide = count // deep
    line, depth = group // deep, group & (deep - 1)

    def hops(offset):
        dx, dz = offset
        return min(dx, wide - dx) + min(dz, deep - dz)

    offsets = sorted(((dx, dz) for dx in range(wide) for dz in range(deep)), key=hops)[::-1]
    offsets = [(0, 0)] + offsets[:-1]

    def group_at(q, sign=1):
        dx, dz = offsets[q]
        dx, dz = (dx, dz) if sign > 0 else (wide - dx, deep - dz)
        return ((line + dx) & (wide - 1)) * deep + ((depth + dz) & (deep - 1))

    def mate(q):
        return base + ((inside + q) & 7)

    def far_mate(q):
        return group_at(q) * 8 + inside

    loads = {}

    def load(**pairs):
        for name, (src, dst) in pairs.items():
            loads[name] = pltpu.make_async_copy(src, dst, load_sem.at[len(loads)])
            loads[name].start()

    load(order=(order_h, order_v), rhs=(rhs_h, rhs_v), lb=(lb_h, lb_v), t1=(t1_h, t1_v))
    load(t2=(t2_h, t2_v), tr=(tr_h, tr_v), tt=(tt_h, tt_v))

    barrier = pltpu.get_barrier_semaphore()

    def greet(device):
        pl.semaphore_signal(barrier, inc=1, device_id=(device,), device_id_type=MESH)

    greet(above)
    greet(below)

    @pl.loop(1, 8)
    def _(q):
        greet(mate(q))

    for q in range(1, count):
        greet(far_mate(q))

    rows, lanes = iota((256, 256), 0), iota((256, 256), 1)

    def natural(place):
        return ((place >> 5) & 3) * 64 + (place & 31) * 2 + (place >> 7)

    to_d[...] = jnp.where(rows == natural(lanes), 1.0, 0.0).astype(BF16)
    to_n[...] = jnp.where(lanes == natural(rows), 1.0, 0.0).astype(BF16)
    diagonal[...] = jnp.where(
        ((iota((64, 256), 1) >> 5) & 3) == (iota((64, 256), 0) >> 4), 1.0, 0.0
    ).astype(BF16)

    loads["rhs"].wait()
    table[...] = table_of([rhs_v[:, 128 * t : 128 * t + 128] for t in range(32)])
    loads["order"].wait()
    split_next = [
        (name, ref, w, g)
        for name, ref, w, groups in (
            ("lb", lb_v, w_lb, 8), ("t1", t1_v, w_t1, 8), ("t2", t2_v, w_t2, 4), ("tr", tr_v, w_tr, 2)
        )
        for g in range(groups)
    ]

    def split_one():
        name, ref, w, g = split_next.pop(0)
        if g == 0:
            loads[name].wait()
        for half in range(2):
            w[g, :, 128 * half : 128 * half + 128] = prepare(ref, g, half)

    for j in range(8):
        row = order_v[:, 512 * j : 512 * j + 512]
        found = lookup(table[...], row >> 7, row & 127)
        for i in range(4):
            tile = found[:, 128 * i : 128 * i + 128]
            tiles[4 * j + i] = tile
            for k, block in enumerate(pair(tile)):
                e_ord[8 * j + 2 * i + k + 1] = e_rows(block)
        for _ in range(min(j + 1, 3)):
            split_one()
    while split_next:
        split_one()
    load(near=(near_h, near_v), fa=(fa_h, fa_v), fb=(fb_h, fb_v), fc=(fc_h, fc_v), tb=(tb_h, tb_v))

    loads["tt"].wait()
    sort = jnp.where(
        iota((64, 64), 0) == (iota((64, 64), 1) & 31) * 2 + (iota((64, 64), 1) >> 5), 1.0, 0.0
    ).astype(F32)

    def top_matrix(j):
        rows = tt_v[j]
        return dot(sort, jnp.concatenate([rows[:, :64], rows[:, 64:]], axis=0), EXACT)

    lift = dot(top_matrix(0), dot(top_matrix(1), top_matrix(2), EXACT), EXACT)
    lift_wide = jnp.concatenate([lift, lift], axis=1)
    lift_tall = jnp.concatenate([lift, lift], axis=0)

    def spread_rows(groups):
        quads = 2 * groups
        x = jnp.concatenate(
            [jnp.concatenate([tiles[2 * q], tiles[2 * q + 1]], axis=1) for q in range(quads)], axis=0
        )
        moved = dot(jnp.concatenate(split(x), axis=0), to_d[...]).astype(BF16)
        dmat[0, 0:quads] = moved[0 : 16 * quads].reshape(quads, 16, 256)
        dmat[1, 0:quads] = moved[16 * quads :].reshape(quads, 16, 256)

    def up_group(g, w):
        mask = diagonal[...]
        lhs = jnp.concatenate(
            [
                jnp.concatenate([dmat[part, 2 * g + half]] * 4, axis=0) * mask
                for half in range(2)
                for part in range(2)
            ],
            axis=0,
        )
        product = dot(lhs, w)
        results = []
        for half in range(2):
            at = slice(128 * half, 128 * half + 128)
            both = product[128 * half : 128 * half + 64, at] + product[128 * half + 64 : 128 * half + 128, at]
            results.append(both + swap(both))
        return jnp.concatenate(results, axis=0)

    def each(groups, unroll, step):
        def body(g, carry):
            step(g)
            return carry

        lax.fori_loop(0, groups, body, 0, unroll=min(unroll, groups))

    halo_down[0] = pack(pair(tiles[0])[0])
    halo_up[0] = pack(pair(tiles[31])[1])

    spread_rows(8)

    def leaf_up(g):
        r = up_group(g, w_lb[g])
        e0[pl.ds(8 * g + 3, 8)] = e_rows(r).reshape(8, 16, 256)
        for i in range(4):
            tiles[4 * g + i] = jnp.where(
                low_half(16), r[32 * i : 32 * i + 16], r[32 * i + 16 : 32 * i + 32]
            )

    each(8, UP_UNROLL, leaf_up)

    def keep_ends(slot, nodes):
        for i in range(3):
            first, last = tiles[i // 2], tiles[(nodes - 3 + i) // 2]
            halo_down[slot + i] = pack(pair(first)[i % 2])
            halo_up[slot + i] = pack(pair(last)[(nodes - 3 + i) % 2])

    keep_ends(1, 64)

    def climb(groups, w_ref, e_ref):
        spread_rows(groups)

        def step(g):
            r = up_group(g, w_ref[g])
            parents = [r[32 * i : 32 * i + 16] + r[32 * i + 16 : 32 * i + 32] for i in range(4)]
            for i in range(2):
                tiles[2 * g + i] = jnp.where(low_half(16), parents[2 * i], parents[2 * i + 1])
            for i in range(4):
                e_ref[4 * g + 3 + i] = e_rows(parents[i])

        each(groups, UP_UNROLL, step)

    climb(8, w_t1, e1)
    keep_ends(4, 32)
    climb(4, w_t2, e2)
    keep_ends(7, 16)

    spread_rows(2)
    rooted = jnp.zeros((16, 128), F32)
    for g in range(2):
        r = up_group(g, w_tr[g])
        for n in range(8):
            rooted = rooted + r[16 * n : 16 * n + 16]
    offered = pack(dot(rooted[:, :64], lift_wide, EXACT))
    a_send[...] = offered
    a_buf[0] = offered

    pl.semaphore_wait(barrier, 2 + 7 + count - 1)

    def remote(src, dst, send, receive, device):
        return pltpu.make_async_remote_copy(
            src_ref=src, dst_ref=dst, send_sem=send, recv_sem=receive,
            device_id=(device,), device_id_type=MESH,
        )

    def a_copy(q):
        return remote(a_send, a_buf.at[q], a_ssem.at[q], a_rsem.at[q], mate(q))

    def b_copy(q):
        return remote(b_send, b_buf.at[group], b_ssem.at[q], b_rsem.at[group], far_mate(q))

    def b_arrival(q):
        origin = group_at(q, -1)
        return remote(b_send, b_buf.at[origin], b_ssem.at[q], b_rsem.at[origin], far_mate(q))

    def c_copy(q):
        return remote(c_send.at[q], c_buf.at[q], c_ssem.at[q], c_rsem.at[q], far_mate(q))

    def d_copy(q):
        return remote(d_send, d_buf.at[q], d_ssem.at[q], d_rsem.at[q], mate(q))

    def over(first, last, action):
        for q in range(first, last):
            action(q)

    over(1, 8, lambda q: a_copy(q).start())
    up_copy = remote(halo_up, from_below, halo_sems.at[0], halo_sems.at[1], above)
    down_copy = remote(halo_down, from_above, halo_sems.at[2], halo_sems.at[3], below)
    up_copy.start()
    down_copy.start()

    find_points(order_v, inverse)
    up_copy.wait_recv()
    down_copy.wait_recv()

    def fill(e_ref, nodes, width, slot):
        for i in range(width):
            lower = jnp.where(me == 0, 0.0, unpack(from_below[slot + i]))
            upper = jnp.where(me == devices - 1, 0.0, unpack(from_above[slot + i]))
            e_ref[i] = e_rows(lower)
            e_ref[nodes + width + i] = e_rows(upper)

    fill(e_ord, 64, 1, 0)
    fill(e0, 64, 3, 1)
    fill(e1, 32, 3, 4)
    fill(e2, 16, 3, 7)

    def partners(g, picks, blocks, e_ref, shift, result):
        for half in range(2):
            lhs, w = [], []
            for s in range(3):
                rows = []
                for n in range(4):
                    node = 8 * g + 4 * half + n
                    rows.append(e_ref[node + shift(picks[s, node])])
                lhs.append(jnp.concatenate(rows, axis=0))
                w.append(prepare(blocks.at[s], g, half))
            result[2 * g + half] = pick_diagonal(times(lhs, w))

    def near_shift(pick):
        return pick + 1

    def far_shift(pick):
        return pick + (pick >> 1) * 3

    def near_part(first):
        each(
            4,
            NEAR_UNROLL,
            lambda g: partners(g + first, near_pick, near_v, e_ord, near_shift, near_f),
        )

    loads["near"].wait()
    near_part(0)

    over(1, 8, lambda q: a_copy(q).wait_recv())

    def total_of(buffer, slots):
        result = buffer[0]
        for q in range(1, slots):
            result = result + buffer[q]
        return result

    summed = total_of(a_buf, 8)
    b_send[...] = summed
    b_buf[group] = summed
    over(1, count, lambda q: b_copy(q).start())

    near_part(4)
    loads["tb"].wait()
    w_top = split_rows([tb_v[pl.ds(n, 32, stride=4), :] for n in range(4)])

    over(1, count, lambda q: b_arrival(q).wait_recv())

    picked = []
    for b in range(4):
        picked.append(e_rows(unpack(b_buf[top_source[b]])))
    coupled = pick_diagonal(times([jnp.concatenate(picked, axis=0)], [w_top]))
    moved = dot(jnp.concatenate(split(coupled), axis=0), to_n[...])
    moved = moved[0:16] + moved[16:32]
    packed = []
    for i in range(2):
        packed += [pack(block) for block in pair(moved[:, 128 * i : 128 * i + 128])]
    for q in range(count):
        target = group_at(q)
        part = jnp.zeros((8, 128), F32)
        for b in range(4):
            part = part + jnp.where(jnp.full((8, 128), top_target[b]) == target, packed[b], 0.0)
        if q == 0:
            c_buf[0] = part
        else:
            c_send[q] = part
    over(1, count, lambda q: c_copy(q).start())

    loads["fa"].wait()
    each(8, NEAR_UNROLL, lambda g: partners(g, pick_a, fa_v, e0, far_shift, far_a))

    over(1, count, lambda q: c_copy(q).wait_recv())
    summed = total_of(c_buf, count)
    d_send[...] = summed
    d_buf[0] = summed
    over(1, 8, lambda q: d_copy(q).start())

    loads["fb"].wait()
    each(4, NEAR_UNROLL, lambda g: partners(g, pick_b, fb_v, e1, far_shift, far_b))
    loads["fc"].wait()
    each(2, NEAR_UNROLL, lambda g: partners(g, pick_c, fc_v, e2, far_shift, far_c))

    over(1, 8, lambda q: d_copy(q).wait_recv())
    falling = unpack(total_of(d_buf, 8))
    root_down = dot_nt(falling[:, :64], lift_tall, EXACT)

    def to_e(values, quads):
        moved = dot(jnp.concatenate(split(values), axis=0), to_n[...])
        rows = 16 * quads
        for q in range(quads):
            for i in range(2):
                at = slice(128 * i, 128 * i + 128)
                heads = pair(moved[16 * q : 16 * q + 16, at])
                rests = pair(moved[rows + 16 * q : rows + 16 * q + 16, at])
                for k in range(2):
                    e_down[4 * q + 2 * i + k] = jnp.concatenate(
                        [heads[k].astype(BF16), rests[k].astype(BF16)], axis=1
                    )

    def half_of(w_ref, g, half):
        return w_ref[g, :, 128 * half : 128 * half + 128]

    root_e = e_rows(root_down)
    values = [
        far_c[2 * g + half] + times([root_e], [half_of(w_tr, g, half)])
        for g in range(2)
        for half in range(2)
    ]
    to_e(jnp.concatenate(values, axis=0), 4)

    def descend(groups, w_ref, far):
        def step(g):
            for half in range(2):
                q = 2 * g + half
                first, second = e_down[2 * q], e_down[2 * q + 1]
                lhs = jnp.concatenate([first, first, second, second], axis=0)
                far[q] = far[q] + pick_diagonal(times([lhs], [half_of(w_ref, g, half)]))

        each(groups, UP_UNROLL, step)
        to_e(jnp.concatenate([far[q] for q in range(2 * groups)], axis=0), 2 * groups)

    descend(4, w_t2, far_b)
    descend(8, w_t1, far_a)

    def leaf_down(g):
        for half in range(2):
            q = 2 * g + half
            lhs = e_down[pl.ds(4 * q, 4)].reshape(64, 256)
            value = near_f[q] + pick_diagonal(times([lhs], [half_of(w_lb, g, half)]))
            for i in range(2):
                vals[2 * q + i] = value[:, 128 * i : 128 * i + 128]

    each(8, UP_UNROLL, leaf_down)

    up_copy.wait_send()
    down_copy.wait_send()
    over(1, 8, lambda q: a_copy(q).wait_send())
    over(1, count, lambda q: b_copy(q).wait_send())
    over(1, count, lambda q: c_copy(q).wait_send())
    over(1, 8, lambda q: d_copy(q).wait_send())


def restore(vals, inverse, out):
    table = table_of([vals[t] for t in range(32)])
    for j in range(8):
        rows = [inverse[4 * j + i : 4 * j + i + 1, :] for i in range(4)]
        lanes = [inverse[4 * j + i + 32 : 4 * j + i + 33, :] for i in range(4)]
        out[:, 512 * j : 512 * j + 512] = lookup(
            table, jnp.concatenate(rows, axis=1), jnp.concatenate(lanes, axis=1)
        )


def lay_out(flat):
    lead, nodes = flat.shape[:-2], flat.shape[-2]
    n = min(nodes, 8)
    rows = jnp.swapaxes(flat.reshape(lead + (nodes // n, n, 32, 128)), -3, -2)
    return rows.reshape(lead + (nodes * 32, 128))


def body(devices, *args):
    smem, hbm = pl.BlockSpec(memory_space=pltpu.SMEM), pl.BlockSpec(memory_space=pl.ANY)
    vm, whole = pltpu.VMEM, pl.BlockSpec(memory_space=pltpu.VMEM)
    args = [lay_out(a) if i in (2, 4, 5, 6, 7, 9, 11, 13, 14, 17) else a for i, a in enumerate(args)]
    small = (3, 8, 10, 12, 15, 16)
    count = devices // 8
    big = [0, 1, 2, 4, 5, 6, 7, 9, 11, 13, 14, 17]
    dma = pltpu.SemaphoreType.DMA
    scratch = [vm(args[i].shape, args[i].dtype) for i in big]
    scratch += [
        vm((8, 256, 256), BF16),
        vm((8, 256, 256), BF16),
        vm((4, 256, 256), BF16),
        vm((2, 256, 256), BF16),
        vm((256, 256), BF16),
        vm((256, 256), BF16),
        vm((64, 256), BF16),
        vm((2, 16, 16, 256), BF16),
        vm((512, 256), BF16),
        vm((32, 16, 128), F32),
        vm((66, 16, 256), BF16),
        vm((70, 16, 256), BF16),
        vm((38, 16, 256), BF16),
        vm((22, 16, 256), BF16),
        vm((64, 16, 256), BF16),
        vm((16, 16, 256), F32),
        vm((16, 16, 256), F32),
        vm((8, 16, 256), F32),
        vm((4, 16, 256), F32),
        vm((10, 8, 128), F32),
        vm((10, 8, 128), F32),
        vm((10, 8, 128), F32),
        vm((10, 8, 128), F32),
        vm((8, 128), F32),
        vm((8, 8, 128), F32),
        vm((8, 128), F32),
        vm((count, 8, 128), F32),
        vm((count, 8, 128), F32),
        vm((count, 8, 128), F32),
        vm((8, 128), F32),
        vm((8, 8, 128), F32),
        dma((12,)),
        dma((4,)),
        dma((8,)),
        dma((8,)),
        dma((count,)),
        dma((count,)),
        dma((count,)),
        dma((count,)),
        dma((8,)),
        dma((8,)),
    ]
    vals, inverse = pl.pallas_call(
        functools.partial(kernel, devices),
        out_shape=(
            jax.ShapeDtypeStruct((32, 16, 128), F32),
            jax.ShapeDtypeStruct((64, 128), I32),
        ),
        in_specs=[smem if i in small else hbm for i in range(18)],
        out_specs=(whole, whole),
        scratch_shapes=scratch,
        compiler_params=pltpu.CompilerParams(
            collective_id=0, has_side_effects=True, vmem_limit_bytes=60 * 1024 * 1024
        ),
    )(*args)
    return pl.pallas_call(
        restore,
        out_shape=jax.ShapeDtypeStruct((16, 4096), F32),
        in_specs=[whole] * 2,
        out_specs=whole,
        compiler_params=pltpu.CompilerParams(vmem_limit_bytes=60 * 1024 * 1024),
    )(vals, inverse)


def solution(mesh):
    split_rows, split_columns = P("leaf", None), P(None, "leaf")
    split_middle = P(None, "leaf", None)
    in_specs = (
        split_columns,
        split_rows,
        split_rows,
        split_columns,
        split_middle,
        split_rows,
        split_rows,
        split_rows,
        split_columns,
        split_middle,
        split_columns,
        split_middle,
        split_columns,
        split_middle,
        split_middle,
        P("leaf"),
        P("leaf"),
        split_rows,
    )
    return jax.shard_map(
        functools.partial(body, mesh.shape["leaf"]),
        mesh=mesh,
        in_specs=in_specs,
        out_specs=split_columns,
        check_vma=False,
    )
```

```python
import functools

import jax
import jax.numpy as jnp
from jax import lax
from jax.experimental import pallas as pl
from jax.experimental.pallas import tpu as pltpu
from jax.sharding import PartitionSpec as P

F32, BF16, I32 = jnp.float32, jnp.bfloat16, jnp.int32
MESH = pl.DeviceIdType.MESH
EXACT = lax.Precision.HIGHEST
NEAR_UNROLL = 2
UP_UNROLL = 8


def iota(shape, dim):
    return lax.broadcasted_iota(I32, shape, dim)


def dot(a, b, precision=None):
    return lax.dot_general(
        a, b, (((1,), (0,)), ((), ())), precision=precision, preferred_element_type=F32
    )


def dot_nt(a, b, precision=None):
    return lax.dot_general(
        a, b, (((1,), (1,)), ((), ())), precision=precision, preferred_element_type=F32
    )


def split(x):
    head = x.astype(BF16)
    return head, (x - head.astype(F32)).astype(BF16)


def low_half(rows):
    return iota((rows, 128), 1) < 64


def swap(x):
    return pltpu.roll(x, 64, 1)


def prepare(ref, g, half):
    start = g * 256 + 4 * half
    return split_rows([ref[pl.ds(start + n, 32, stride=8), :] for n in range(4)])


def split_rows(matrices):
    a = jnp.concatenate(matrices, axis=0)
    head = a.astype(BF16)
    rest = (a - head.astype(F32)).astype(BF16)
    low = low_half(128)
    top = jnp.where(low, head, swap(rest))
    bottom = jnp.where(low, swap(head), rest)
    return jnp.concatenate([top, bottom], axis=0)


def pack(block):
    return jnp.where(low_half(8), block[0:8], block[8:16])


def unpack(packed):
    low, other = low_half(8), swap(packed)
    return jnp.concatenate(
        [jnp.where(low, packed, other), jnp.where(low, other, packed)], axis=0
    )


def pair(tile):
    low, other = low_half(16), swap(tile)
    return jnp.where(low, tile, other), jnp.where(low, other, tile)


def e_rows(block):
    head, rest = split(block)
    return jnp.concatenate([head, rest], axis=1)


def pick_diagonal(wide):
    lane_node = (iota((16, 256), 1) >> 5) & 3
    result = wide[0:16]
    for n in range(1, 4):
        result = jnp.where(lane_node == n, wide[16 * n : 16 * n + 16], result)
    return result


def table_of(tiles):
    head, rest = split(jnp.concatenate(tiles, axis=0))
    return jnp.concatenate([head, rest], axis=1)


def lookup(table, tile_index, lane_index):
    width = lane_index.shape[1]
    hot = jnp.where(iota((128, width), 0) == lane_index, 1.0, 0.0).astype(BF16)
    found = dot(table, jnp.concatenate([hot, hot], axis=0))
    tile_index = jnp.broadcast_to(tile_index, (16, width))
    result = found[0:16]
    for s in range(1, 32):
        result = jnp.where(tile_index == s, found[16 * s : 16 * s + 16], result)
    return result


def find_points(order, inverse):
    def step(j, total):
        row = order[:, pl.ds(pl.multiple_of(j * 512, 512), 512)]
        lane = iota((1, 512), 1)
        n, p = lane >> 6, lane & 63
        parity, c = p & 1, p >> 1
        tile = (j * 4 + (n >> 2) * 2 + parity).astype(F32)
        place = ((n & 3) * 32 + c).astype(F32)
        chosen = iota((32, 512), 0) == (row >> 7)
        rows = jnp.concatenate(
            [jnp.where(chosen, tile, 0.0), jnp.where(chosen, place, 0.0)], axis=0
        ).astype(BF16)
        columns = jnp.where(iota((128, 512), 0) == (row & 127), 1.0, 0.0).astype(BF16)
        return total + dot_nt(rows, columns)

    inverse[...] = lax.fori_loop(0, 8, step, jnp.zeros((64, 128), F32), unroll=2).astype(I32)


def times(lhs_terms, w_terms):
    rows = lhs_terms[0].shape[0]
    heads = jnp.concatenate([lhs[:, :128] for lhs in lhs_terms], axis=1)
    rests = jnp.concatenate([lhs[:, 128:] for lhs in lhs_terms], axis=1)
    both = dot_nt(jnp.concatenate([heads, rests], axis=0), jnp.concatenate(w_terms, axis=1))
    return both[:rows] + both[rows:]


def kernel(
    devices,
    rhs_h, order_h, lb_h, near_pick, near_h, t1_h, t2_h, tr_h,
    pick_a, fa_h, pick_b, fb_h, pick_c, fc_h, tt_h, top_source, top_target, tb_h,
    vals, inverse,
    rhs_v, order_v, lb_v, near_v, t1_v, t2_v, tr_v, fa_v, fb_v, fc_v, tt_v, tb_v,
    w_lb, w_t1, w_t2, w_tr, to_d, to_n, diagonal, dmat, table, tiles,
    e_ord, e0, e1, e2, e_down, near_f, far_a, far_b, far_c,
    halo_up, halo_down, from_below, from_above,
    a_send, a_buf, b_send, b_buf, c_send, c_buf, d_send, d_buf,
    load_sem, halo_sems, a_ssem, a_rsem, b_ssem, b_rsem, c_ssem, c_rsem, d_ssem, d_rsem,
):
    me = lax.axis_index("leaf")
    count = devices // 8
    inside, group = me & 7, me >> 3
    base = me - inside
    above, below = (me + 1) & (devices - 1), (me + devices - 1) & (devices - 1)
    deep = min(8, count)
    wide = count // deep
    line, depth = group // deep, group & (deep - 1)

    def hops(offset):
        dx, dz = offset
        return min(dx, wide - dx) + min(dz, deep - dz)

    offsets = sorted(((dx, dz) for dx in range(wide) for dz in range(deep)), key=hops)[::-1]
    offsets = [(0, 0)] + offsets[:-1]

    def group_at(q, sign=1):
        dx, dz = offsets[q]
        dx, dz = (dx, dz) if sign > 0 else (wide - dx, deep - dz)
        return ((line + dx) & (wide - 1)) * deep + ((depth + dz) & (deep - 1))

    def mate(q):
        return base + ((inside + q) & 7)

    def far_mate(q):
        return group_at(q) * 8 + inside

    loads = {}

    def load(**pairs):
        for name, (src, dst) in pairs.items():
            loads[name] = pltpu.make_async_copy(src, dst, load_sem.at[len(loads)])
            loads[name].start()

    load(order=(order_h, order_v), rhs=(rhs_h, rhs_v), lb=(lb_h, lb_v), t1=(t1_h, t1_v))
    load(t2=(t2_h, t2_v), tr=(tr_h, tr_v), tt=(tt_h, tt_v))

    barrier = pltpu.get_barrier_semaphore()

    def greet(device):
        pl.semaphore_signal(barrier, inc=1, device_id=(device,), device_id_type=MESH)

    greet(above)
    greet(below)

    @pl.loop(1, 8)
    def _(q):
        greet(mate(q))

    for q in range(1, count):
        greet(far_mate(q))

    rows, lanes = iota((256, 256), 0), iota((256, 256), 1)

    def natural(place):
        return ((place >> 5) & 3) * 64 + (place & 31) * 2 + (place >> 7)

    to_d[...] = jnp.where(rows == natural(lanes), 1.0, 0.0).astype(BF16)
    to_n[...] = jnp.where(lanes == natural(rows), 1.0, 0.0).astype(BF16)
    diagonal[...] = jnp.where(
        ((iota((64, 256), 1) >> 5) & 3) == (iota((64, 256), 0) >> 4), 1.0, 0.0
    ).astype(BF16)

    loads["rhs"].wait()
    table[...] = table_of([rhs_v[:, 128 * t : 128 * t + 128] for t in range(32)])
    loads["order"].wait()
    split_next = [
        (name, ref, w, g)
        for name, ref, w, groups in (
            ("lb", lb_v, w_lb, 8), ("t1", t1_v, w_t1, 8), ("t2", t2_v, w_t2, 4), ("tr", tr_v, w_tr, 2)
        )
        for g in range(groups)
    ]

    def split_one():
        name, ref, w, g = split_next.pop(0)
        if g == 0:
            loads[name].wait()
        for half in range(2):
            w[g, :, 128 * half : 128 * half + 128] = prepare(ref, g, half)

    for j in range(8):
        row = order_v[:, 512 * j : 512 * j + 512]
        found = lookup(table[...], row >> 7, row & 127)
        for i in range(4):
            tile = found[:, 128 * i : 128 * i + 128]
            tiles[4 * j + i] = tile
            for k, block in enumerate(pair(tile)):
                e_ord[8 * j + 2 * i + k + 1] = e_rows(block)
        for _ in range(min(j + 1, 3)):
            split_one()
    while split_next:
        split_one()
    load(near=(near_h, near_v), fa=(fa_h, fa_v), fb=(fb_h, fb_v), fc=(fc_h, fc_v), tb=(tb_h, tb_v))

    loads["tt"].wait()
    sort = jnp.where(
        iota((64, 64), 0) == (iota((64, 64), 1) & 31) * 2 + (iota((64, 64), 1) >> 5), 1.0, 0.0
    ).astype(F32)

    def top_matrix(j):
        rows = tt_v[j]
        return dot(sort, jnp.concatenate([rows[:, :64], rows[:, 64:]], axis=0), EXACT)

    lift = dot(top_matrix(0), dot(top_matrix(1), top_matrix(2), EXACT), EXACT)
    lift_wide = jnp.concatenate([lift, lift], axis=1)
    lift_tall = jnp.concatenate([lift, lift], axis=0)

    def spread_rows(groups):
        quads = 2 * groups
        x = jnp.concatenate(
            [jnp.concatenate([tiles[2 * q], tiles[2 * q + 1]], axis=1) for q in range(quads)], axis=0
        )
        moved = dot(jnp.concatenate(split(x), axis=0), to_d[...]).astype(BF16)
        dmat[0, 0:quads] = moved[0 : 16 * quads].reshape(quads, 16, 256)
        dmat[1, 0:quads] = moved[16 * quads :].reshape(quads, 16, 256)

    def up_group(g, w):
        mask = diagonal[...]
        lhs = jnp.concatenate(
            [
                jnp.concatenate([dmat[part, 2 * g + half]] * 4, axis=0) * mask
                for half in range(2)
                for part in range(2)
            ],
            axis=0,
        )
        product = dot(lhs, w)
        results = []
        for half in range(2):
            at = slice(128 * half, 128 * half + 128)
            both = product[128 * half : 128 * half + 64, at] + product[128 * half + 64 : 128 * half + 128, at]
            results.append(both + swap(both))
        return jnp.concatenate(results, axis=0)

    def each(groups, unroll, step):
        def body(g, carry):
            step(g)
            return carry

        lax.fori_loop(0, groups, body, 0, unroll=min(unroll, groups))

    halo_down[0] = pack(pair(tiles[0])[0])
    halo_up[0] = pack(pair(tiles[31])[1])

    spread_rows(8)

    def leaf_up(g):
        r = up_group(g, w_lb[g])
        e0[pl.ds(8 * g + 3, 8)] = e_rows(r).reshape(8, 16, 256)
        for i in range(4):
            tiles[4 * g + i] = jnp.where(
                low_half(16), r[32 * i : 32 * i + 16], r[32 * i + 16 : 32 * i + 32]
            )

    each(8, UP_UNROLL, leaf_up)

    def keep_ends(slot, nodes):
        for i in range(3):
            first, last = tiles[i // 2], tiles[(nodes - 3 + i) // 2]
            halo_down[slot + i] = pack(pair(first)[i % 2])
            halo_up[slot + i] = pack(pair(last)[(nodes - 3 + i) % 2])

    keep_ends(1, 64)

    def climb(groups, w_ref, e_ref):
        spread_rows(groups)

        def step(g):
            r = up_group(g, w_ref[g])
            parents = [r[32 * i : 32 * i + 16] + r[32 * i + 16 : 32 * i + 32] for i in range(4)]
            for i in range(2):
                tiles[2 * g + i] = jnp.where(low_half(16), parents[2 * i], parents[2 * i + 1])
            for i in range(4):
                e_ref[4 * g + 3 + i] = e_rows(parents[i])

        each(groups, UP_UNROLL, step)

    climb(8, w_t1, e1)
    keep_ends(4, 32)
    climb(4, w_t2, e2)
    keep_ends(7, 16)

    spread_rows(2)
    rooted = jnp.zeros((16, 128), F32)
    for g in range(2):
        r = up_group(g, w_tr[g])
        for n in range(8):
            rooted = rooted + r[16 * n : 16 * n + 16]
    offered = pack(dot(rooted[:, :64], lift_wide, EXACT))
    a_send[...] = offered
    a_buf[0] = offered

    pl.semaphore_wait(barrier, 2 + 7 + count - 1)

    def remote(src, dst, send, receive, device):
        return pltpu.make_async_remote_copy(
            src_ref=src, dst_ref=dst, send_sem=send, recv_sem=receive,
            device_id=(device,), device_id_type=MESH,
        )

    def a_copy(q):
        return remote(a_send, a_buf.at[q], a_ssem.at[q], a_rsem.at[q], mate(q))

    def b_copy(q):
        return remote(b_send, b_buf.at[group], b_ssem.at[q], b_rsem.at[group], far_mate(q))

    def b_arrival(q):
        origin = group_at(q, -1)
        return remote(b_send, b_buf.at[origin], b_ssem.at[q], b_rsem.at[origin], far_mate(q))

    def c_copy(q):
        return remote(c_send.at[q], c_buf.at[q], c_ssem.at[q], c_rsem.at[q], far_mate(q))

    def d_copy(q):
        return remote(d_send, d_buf.at[q], d_ssem.at[q], d_rsem.at[q], mate(q))

    def over(first, last, action):
        for q in range(first, last):
            action(q)

    over(1, 8, lambda q: a_copy(q).start())
    up_copy = remote(halo_up, from_below, halo_sems.at[0], halo_sems.at[1], above)
    down_copy = remote(halo_down, from_above, halo_sems.at[2], halo_sems.at[3], below)
    up_copy.start()
    down_copy.start()

    find_points(order_v, inverse)
    up_copy.wait_recv()
    down_copy.wait_recv()

    def fill(e_ref, nodes, width, slot):
        for i in range(width):
            lower = jnp.where(me == 0, 0.0, unpack(from_below[slot + i]))
            upper = jnp.where(me == devices - 1, 0.0, unpack(from_above[slot + i]))
            e_ref[i] = e_rows(lower)
            e_ref[nodes + width + i] = e_rows(upper)

    fill(e_ord, 64, 1, 0)
    fill(e0, 64, 3, 1)
    fill(e1, 32, 3, 4)
    fill(e2, 16, 3, 7)

    def partners(g, picks, blocks, e_ref, shift, result):
        for half in range(2):
            lhs, w = [], []
            for s in range(3):
                rows = []
                for n in range(4):
                    node = 8 * g + 4 * half + n
                    rows.append(e_ref[node + shift(picks[s, node])])
                lhs.append(jnp.concatenate(rows, axis=0))
                w.append(prepare(blocks.at[s], g, half))
            result[2 * g + half] = pick_diagonal(times(lhs, w))

    def near_shift(pick):
        return pick + 1

    def far_shift(pick):
        return pick + (pick >> 1) * 3

    def near_part(first):
        each(
            4,
            NEAR_UNROLL,
            lambda g: partners(g + first, near_pick, near_v, e_ord, near_shift, near_f),
        )

    loads["near"].wait()
    near_part(0)

    over(1, 8, lambda q: a_copy(q).wait_recv())

    def total_of(buffer, slots):
        result = buffer[0]
        for q in range(1, slots):
            result = result + buffer[q]
        return result

    summed = total_of(a_buf, 8)
    b_send[...] = summed
    b_buf[group] = summed
    over(1, count, lambda q: b_copy(q).start())

    near_part(4)
    loads["tb"].wait()
    w_top = split_rows([tb_v[pl.ds(n, 32, stride=4), :] for n in range(4)])

    over(1, count, lambda q: b_arrival(q).wait_recv())

    picked = []
    for b in range(4):
        picked.append(e_rows(unpack(b_buf[top_source[b]])))
    coupled = pick_diagonal(times([jnp.concatenate(picked, axis=0)], [w_top]))
    moved = dot(jnp.concatenate(split(coupled), axis=0), to_n[...])
    moved = moved[0:16] + moved[16:32]
    packed = []
    for i in range(2):
        packed += [pack(block) for block in pair(moved[:, 128 * i : 128 * i + 128])]
    for q in range(count):
        target = group_at(q)
        part = jnp.zeros((8, 128), F32)
        for b in range(4):
            part = part + jnp.where(jnp.full((8, 128), top_target[b]) == target, packed[b], 0.0)
        if q == 0:
            c_buf[0] = part
        else:
            c_send[q] = part
    over(1, count, lambda q: c_copy(q).start())

    loads["fa"].wait()
    each(8, NEAR_UNROLL, lambda g: partners(g, pick_a, fa_v, e0, far_shift, far_a))

    over(1, count, lambda q: c_copy(q).wait_recv())
    summed = total_of(c_buf, count)
    d_send[...] = summed
    d_buf[0] = summed
    over(1, 8, lambda q: d_copy(q).start())

    loads["fb"].wait()
    each(4, NEAR_UNROLL, lambda g: partners(g, pick_b, fb_v, e1, far_shift, far_b))
    loads["fc"].wait()
    each(2, NEAR_UNROLL, lambda g: partners(g, pick_c, fc_v, e2, far_shift, far_c))

    over(1, 8, lambda q: d_copy(q).wait_recv())
    falling = unpack(total_of(d_buf, 8))
    root_down = dot_nt(falling[:, :64], lift_tall, EXACT)

    def to_e(values, quads):
        moved = dot(jnp.concatenate(split(values), axis=0), to_n[...])
        rows = 16 * quads
        for q in range(quads):
            for i in range(2):
                at = slice(128 * i, 128 * i + 128)
                heads = pair(moved[16 * q : 16 * q + 16, at])
                rests = pair(moved[rows + 16 * q : rows + 16 * q + 16, at])
                for k in range(2):
                    e_down[4 * q + 2 * i + k] = jnp.concatenate(
                        [heads[k].astype(BF16), rests[k].astype(BF16)], axis=1
                    )

    def half_of(w_ref, g, half):
        return w_ref[g, :, 128 * half : 128 * half + 128]

    root_e = e_rows(root_down)
    values = [
        far_c[2 * g + half] + times([root_e], [half_of(w_tr, g, half)])
        for g in range(2)
        for half in range(2)
    ]
    to_e(jnp.concatenate(values, axis=0), 4)

    def descend(groups, w_ref, far):
        def step(g):
            for half in range(2):
                q = 2 * g + half
                first, second = e_down[2 * q], e_down[2 * q + 1]
                lhs = jnp.concatenate([first, first, second, second], axis=0)
                far[q] = far[q] + pick_diagonal(times([lhs], [half_of(w_ref, g, half)]))

        each(groups, UP_UNROLL, step)
        to_e(jnp.concatenate([far[q] for q in range(2 * groups)], axis=0), 2 * groups)

    descend(4, w_t2, far_b)
    descend(8, w_t1, far_a)

    def leaf_down(g):
        for half in range(2):
            q = 2 * g + half
            lhs = e_down[pl.ds(4 * q, 4)].reshape(64, 256)
            value = near_f[q] + pick_diagonal(times([lhs], [half_of(w_lb, g, half)]))
            for i in range(2):
                vals[2 * q + i] = value[:, 128 * i : 128 * i + 128]

    each(8, UP_UNROLL, leaf_down)

    up_copy.wait_send()
    down_copy.wait_send()
    over(1, 8, lambda q: a_copy(q).wait_send())
    over(1, count, lambda q: b_copy(q).wait_send())
    over(1, count, lambda q: c_copy(q).wait_send())
    over(1, 8, lambda q: d_copy(q).wait_send())


def restore(vals, inverse, out):
    table = table_of([vals[t] for t in range(32)])
    for j in range(8):
        rows = [inverse[4 * j + i : 4 * j + i + 1, :] for i in range(4)]
        lanes = [inverse[4 * j + i + 32 : 4 * j + i + 33, :] for i in range(4)]
        out[:, 512 * j : 512 * j + 512] = lookup(
            table, jnp.concatenate(rows, axis=1), jnp.concatenate(lanes, axis=1)
        )


def lay_out(flat):
    lead, nodes = flat.shape[:-2], flat.shape[-2]
    n = min(nodes, 8)
    rows = jnp.swapaxes(flat.reshape(lead + (nodes // n, n, 32, 128)), -3, -2)
    return rows.reshape(lead + (nodes * 32, 128))


def body(devices, *args):
    smem, hbm = pl.BlockSpec(memory_space=pltpu.SMEM), pl.BlockSpec(memory_space=pl.ANY)
    vm, whole = pltpu.VMEM, pl.BlockSpec(memory_space=pltpu.VMEM)
    args = [lay_out(a) if i in (2, 4, 5, 6, 7, 9, 11, 13, 14, 17) else a for i, a in enumerate(args)]
    small = (3, 8, 10, 12, 15, 16)
    count = devices // 8
    big = [0, 1, 2, 4, 5, 6, 7, 9, 11, 13, 14, 17]
    dma = pltpu.SemaphoreType.DMA
    scratch = [vm(args[i].shape, args[i].dtype) for i in big]
    scratch += [
        vm((8, 256, 256), BF16),
        vm((8, 256, 256), BF16),
        vm((4, 256, 256), BF16),
        vm((2, 256, 256), BF16),
        vm((256, 256), BF16),
        vm((256, 256), BF16),
        vm((64, 256), BF16),
        vm((2, 16, 16, 256), BF16),
        vm((512, 256), BF16),
        vm((32, 16, 128), F32),
        vm((66, 16, 256), BF16),
        vm((70, 16, 256), BF16),
        vm((38, 16, 256), BF16),
        vm((22, 16, 256), BF16),
        vm((64, 16, 256), BF16),
        vm((16, 16, 256), F32),
        vm((16, 16, 256), F32),
        vm((8, 16, 256), F32),
        vm((4, 16, 256), F32),
        vm((10, 8, 128), F32),
        vm((10, 8, 128), F32),
        vm((10, 8, 128), F32),
        vm((10, 8, 128), F32),
        vm((8, 128), F32),
        vm((8, 8, 128), F32),
        vm((8, 128), F32),
        vm((count, 8, 128), F32),
        vm((count, 8, 128), F32),
        vm((count, 8, 128), F32),
        vm((8, 128), F32),
        vm((8, 8, 128), F32),
        dma((12,)),
        dma((4,)),
        dma((8,)),
        dma((8,)),
        dma((count,)),
        dma((count,)),
        dma((count,)),
        dma((count,)),
        dma((8,)),
        dma((8,)),
    ]
    vals, inverse = pl.pallas_call(
        functools.partial(kernel, devices),
        out_shape=(
            jax.ShapeDtypeStruct((32, 16, 128), F32),
            jax.ShapeDtypeStruct((64, 128), I32),
        ),
        in_specs=[smem if i in small else hbm for i in range(18)],
        out_specs=(whole, whole),
        scratch_shapes=scratch,
        compiler_params=pltpu.CompilerParams(
            collective_id=0, has_side_effects=True, vmem_limit_bytes=60 * 1024 * 1024
        ),
    )(*args)
    return pl.pallas_call(
        restore,
        out_shape=jax.ShapeDtypeStruct((16, 4096), F32),
        in_specs=[whole] * 2,
        out_specs=whole,
        compiler_params=pltpu.CompilerParams(vmem_limit_bytes=60 * 1024 * 1024),
    )(vals, inverse)


def solution(mesh):
    split_rows, split_columns = P("leaf", None), P(None, "leaf")
    split_middle = P(None, "leaf", None)
    in_specs = (
        split_columns,
        split_rows,
        split_rows,
        split_columns,
        split_middle,
        split_rows,
        split_rows,
        split_rows,
        split_columns,
        split_middle,
        split_columns,
        split_middle,
        split_columns,
        split_middle,
        split_middle,
        P("leaf"),
        P("leaf"),
        split_rows,
    )
    return jax.shard_map(
        functools.partial(body, mesh.shape["leaf"]),
        mesh=mesh,
        in_specs=in_specs,
        out_specs=split_columns,
        check_vma=False,
    )
```

```python
import functools

import jax
import jax.numpy as jnp
from jax import lax
from jax.experimental import pallas as pl
from jax.experimental.pallas import tpu as pltpu
from jax.sharding import PartitionSpec as P

F32, BF16, I32 = jnp.float32, jnp.bfloat16, jnp.int32
MESH = pl.DeviceIdType.MESH
EXACT = lax.Precision.HIGHEST
NEAR_UNROLL = 2
UP_UNROLL = 8
DOWN_UNROLL = 4
Z_UNROLL = 2


def iota(shape, dim):
    return lax.broadcasted_iota(I32, shape, dim)


def dot(a, b, precision=None):
    return lax.dot_general(
        a, b, (((1,), (0,)), ((), ())), precision=precision, preferred_element_type=F32
    )


def dot_nt(a, b, precision=None):
    return lax.dot_general(
        a, b, (((1,), (1,)), ((), ())), precision=precision, preferred_element_type=F32
    )


def split(x):
    head = x.astype(BF16)
    return head, (x - head.astype(F32)).astype(BF16)


def low_half(rows):
    return iota((rows, 128), 1) < 64


def swap(x):
    return pltpu.roll(x, 64, 1)


def prepare(ref, g, half):
    start = g * 256 + 4 * half
    return split_rows([ref[pl.ds(start + n, 32, stride=8), :] for n in range(4)])


def split_rows(matrices):
    a = jnp.concatenate(matrices, axis=0)
    head = a.astype(BF16)
    rest = (a - head.astype(F32)).astype(BF16)
    low = low_half(128)
    top = jnp.where(low, head, swap(rest))
    bottom = jnp.where(low, swap(head), rest)
    return jnp.concatenate([top, bottom], axis=0)


def pack(block):
    return jnp.where(low_half(8), block[0:8], block[8:16])


def unpack(packed):
    low, other = low_half(8), swap(packed)
    return jnp.concatenate(
        [jnp.where(low, packed, other), jnp.where(low, other, packed)], axis=0
    )


def pair(tile):
    low, other = low_half(tile.shape[0]), swap(tile)
    return jnp.where(low, tile, other), jnp.where(low, other, tile)


def e_rows(block):
    head, rest = split(block)
    return jnp.concatenate([head, rest], axis=1)


def pick_diagonal(wide, rows=16):
    lane_node = (iota((rows, 256), 1) >> 5) & 3
    result = wide[0:rows]
    for n in range(1, 4):
        result = jnp.where(lane_node == n, wide[rows * n : rows * n + rows], result)
    return result


def table_of(tiles):
    head, rest = split(jnp.concatenate(tiles, axis=0))
    return jnp.concatenate([head, rest], axis=1)


def lookup(table, tile_index, lane_index):
    width = lane_index.shape[1]
    hot = jnp.where(iota((128, width), 0) == lane_index, 1.0, 0.0).astype(BF16)
    found = dot(table, jnp.concatenate([hot, hot], axis=0))
    tile_index = jnp.broadcast_to(tile_index, (16, width))
    result = found[0:16]
    for s in range(1, 32):
        result = jnp.where(tile_index == s, found[16 * s : 16 * s + 16], result)
    return result


def find_points(order, inverse):
    def step(j, total):
        row = order[:, pl.ds(pl.multiple_of(j * 512, 512), 512)]
        lane = iota((1, 512), 1)
        n, p = lane >> 6, lane & 63
        parity, c = p & 1, p >> 1
        tile = (j * 4 + (n >> 2) * 2 + parity).astype(F32)
        place = ((n & 3) * 32 + c).astype(F32)
        chosen = iota((32, 512), 0) == (row >> 7)
        rows = jnp.concatenate(
            [jnp.where(chosen, tile, 0.0), jnp.where(chosen, place, 0.0)], axis=0
        ).astype(BF16)
        columns = jnp.where(iota((128, 512), 0) == (row & 127), 1.0, 0.0).astype(BF16)
        return total + dot_nt(rows, columns)

    inverse[...] = lax.fori_loop(0, 8, step, jnp.zeros((64, 128), F32), unroll=2).astype(I32)


def times(lhs_terms, w_terms):
    rows = lhs_terms[0].shape[0]
    heads = jnp.concatenate([lhs[:, :128] for lhs in lhs_terms], axis=1)
    rests = jnp.concatenate([lhs[:, 128:] for lhs in lhs_terms], axis=1)
    both = dot_nt(jnp.concatenate([heads, rests], axis=0), jnp.concatenate(w_terms, axis=1))
    return both[:rows] + both[rows:]


def kernel(
    devices,
    rhs_h, order_h, lb_h, near_pick, near_h, t1_h, t2_h, tr_h,
    pick_a, fa_h, pick_b, fb_h, pick_c, fc_h, tt_h, top_source, top_target, tb_h,
    vals, inverse,
    rhs_v, order_v, lb_v, near_v, t1_v, t2_v, tr_v, fa_v, fb_v, fc_v, tt_v, tb_v,
    w_lb, w_t1, w_t2, w_tr, to_d, to_n, diagonal, dmat, table, tiles,
    e_ord, e0, e1, e2, e_down, z_d, z_e, z_w, near_f, far_a, far_b, far_c,
    halo_up, halo_down, from_below, from_above,
    a_send, a_buf, b_send, b_buf, c_send, c_buf, d_send, d_buf,
    load_sem, halo_sems, a_ssem, a_rsem, b_ssem, b_rsem, c_ssem, c_rsem, d_ssem, d_rsem,
):
    me = lax.axis_index("leaf")
    count = devices // 8
    inside, group = me & 7, me >> 3
    base = me - inside
    above, below = (me + 1) & (devices - 1), (me + devices - 1) & (devices - 1)
    deep = min(8, count)
    wide = count // deep
    line, depth = group // deep, group & (deep - 1)

    def hops(offset):
        dx, dz = offset
        return min(dx, wide - dx) + min(dz, deep - dz)

    offsets = sorted(((dx, dz) for dx in range(wide) for dz in range(deep)), key=hops)[::-1]
    offsets = [(0, 0)] + offsets[:-1]

    def group_at(q, sign=1):
        dx, dz = offsets[q]
        dx, dz = (dx, dz) if sign > 0 else (wide - dx, deep - dz)
        return ((line + dx) & (wide - 1)) * deep + ((depth + dz) & (deep - 1))

    def mate(q):
        return base + ((inside + q) & 7)

    def far_mate(q):
        return group_at(q) * 8 + inside

    loads = {}

    def load(**pairs):
        for name, (src, dst) in pairs.items():
            loads[name] = pltpu.make_async_copy(src, dst, load_sem.at[len(loads)])
            loads[name].start()

    load(order=(order_h, order_v), rhs=(rhs_h, rhs_v), lb=(lb_h, lb_v), t1=(t1_h, t1_v))
    load(t2=(t2_h, t2_v), tr=(tr_h, tr_v), tt=(tt_h, tt_v))

    barrier = pltpu.get_barrier_semaphore()

    def greet(device):
        pl.semaphore_signal(barrier, inc=1, device_id=(device,), device_id_type=MESH)

    greet(above)
    greet(below)

    @pl.loop(1, 8)
    def _(q):
        greet(mate(q))

    for q in range(1, count):
        greet(far_mate(q))

    rows, lanes = iota((256, 256), 0), iota((256, 256), 1)

    def natural(place):
        return ((place >> 5) & 3) * 64 + (place & 31) * 2 + (place >> 7)

    to_d[...] = jnp.where(rows == natural(lanes), 1.0, 0.0).astype(BF16)
    to_n[...] = jnp.where(lanes == natural(rows), 1.0, 0.0).astype(BF16)
    diagonal[...] = jnp.where(
        ((iota((64, 256), 1) >> 5) & 3) == (iota((64, 256), 0) >> 4), 1.0, 0.0
    ).astype(BF16)

    loads["rhs"].wait()
    table[...] = table_of([rhs_v[:, 128 * t : 128 * t + 128] for t in range(32)])
    loads["order"].wait()
    split_next = [
        (name, ref, w, g)
        for name, ref, w, groups in (
            ("lb", lb_v, w_lb, 8), ("t1", t1_v, w_t1, 8), ("t2", t2_v, w_t2, 4), ("tr", tr_v, w_tr, 2)
        )
        for g in range(groups)
    ]

    def split_one():
        name, ref, w, g = split_next.pop(0)
        if g == 0:
            loads[name].wait()
        for half in range(2):
            w[g, :, 128 * half : 128 * half + 128] = prepare(ref, g, half)

    for j in range(8):
        row = order_v[:, 512 * j : 512 * j + 512]
        found = lookup(table[...], row >> 7, row & 127)
        for i in range(4):
            tile = found[:, 128 * i : 128 * i + 128]
            tiles[4 * j + i] = tile
            for k, block in enumerate(pair(tile)):
                e_ord[8 * j + 2 * i + k + 1] = e_rows(block)
        for _ in range(min(j + 1, 3)):
            split_one()
    while split_next:
        split_one()
    load(near=(near_h, near_v), fa=(fa_h, fa_v), fb=(fb_h, fb_v), fc=(fc_h, fc_v), tb=(tb_h, tb_v))

    loads["tt"].wait()
    sort = jnp.where(
        iota((64, 64), 0) == (iota((64, 64), 1) & 31) * 2 + (iota((64, 64), 1) >> 5), 1.0, 0.0
    ).astype(F32)

    def top_matrix(j):
        rows = tt_v[j]
        return dot(sort, jnp.concatenate([rows[:, :64], rows[:, 64:]], axis=0), EXACT)

    lift = dot(top_matrix(0), dot(top_matrix(1), top_matrix(2), EXACT), EXACT)
    lift_wide = jnp.concatenate([lift, lift], axis=1)

    def spread_rows(groups):
        quads = 2 * groups
        x = jnp.concatenate(
            [jnp.concatenate([tiles[2 * q], tiles[2 * q + 1]], axis=1) for q in range(quads)], axis=0
        )
        moved = dot(jnp.concatenate(split(x), axis=0), to_d[...]).astype(BF16)
        dmat[0, 0:quads] = moved[0 : 16 * quads].reshape(quads, 16, 256)
        dmat[1, 0:quads] = moved[16 * quads :].reshape(quads, 16, 256)

    def up_group(g, w):
        mask = diagonal[...]
        lhs = jnp.concatenate(
            [
                jnp.concatenate([dmat[part, 2 * g + half]] * 4, axis=0) * mask
                for half in range(2)
                for part in range(2)
            ],
            axis=0,
        )
        product = dot(lhs, w)
        results = []
        for half in range(2):
            at = slice(128 * half, 128 * half + 128)
            both = product[128 * half : 128 * half + 64, at] + product[128 * half + 64 : 128 * half + 128, at]
            results.append(both + swap(both))
        return jnp.concatenate(results, axis=0)

    def each(groups, unroll, step):
        def body(g, carry):
            step(g)
            return carry

        lax.fori_loop(0, groups, body, 0, unroll=min(unroll, groups))

    halo_down[0] = pack(pair(tiles[0])[0])
    halo_up[0] = pack(pair(tiles[31])[1])

    spread_rows(8)

    def leaf_up(g):
        r = up_group(g, w_lb[g])
        e0[pl.ds(8 * g + 3, 8)] = e_rows(r).reshape(8, 16, 256)
        for i in range(4):
            tiles[4 * g + i] = jnp.where(
                low_half(16), r[32 * i : 32 * i + 16], r[32 * i + 16 : 32 * i + 32]
            )

    each(8, UP_UNROLL, leaf_up)

    def keep_ends(slot, nodes):
        for i in range(3):
            first, last = tiles[i // 2], tiles[(nodes - 3 + i) // 2]
            halo_down[slot + i] = pack(pair(first)[i % 2])
            halo_up[slot + i] = pack(pair(last)[(nodes - 3 + i) % 2])

    keep_ends(1, 64)

    def climb(groups, w_ref, e_ref):
        spread_rows(groups)

        def step(g):
            r = up_group(g, w_ref[g])
            parents = [r[32 * i : 32 * i + 16] + r[32 * i + 16 : 32 * i + 32] for i in range(4)]
            for i in range(2):
                tiles[2 * g + i] = jnp.where(low_half(16), parents[2 * i], parents[2 * i + 1])
            for i in range(4):
                e_ref[4 * g + 3 + i] = e_rows(parents[i])

        each(groups, UP_UNROLL, step)

    climb(8, w_t1, e1)
    keep_ends(4, 32)
    climb(4, w_t2, e2)
    keep_ends(7, 16)

    spread_rows(2)
    rooted = jnp.zeros((16, 128), F32)
    for g in range(2):
        r = up_group(g, w_tr[g])
        for n in range(8):
            rooted = rooted + r[16 * n : 16 * n + 16]
    offered = pack(dot(rooted[:, :64], lift_wide, EXACT))
    a_send[...] = offered
    a_buf[0] = offered

    pl.semaphore_wait(barrier, 2 + 7 + count - 1)

    def remote(src, dst, send, receive, device):
        return pltpu.make_async_remote_copy(
            src_ref=src, dst_ref=dst, send_sem=send, recv_sem=receive,
            device_id=(device,), device_id_type=MESH,
        )

    def a_copy(q):
        return remote(a_send, a_buf.at[q], a_ssem.at[q], a_rsem.at[q], mate(q))

    def b_copy(q):
        return remote(b_send, b_buf.at[group], b_ssem.at[q], b_rsem.at[group], far_mate(q))

    def b_arrival(q):
        origin = group_at(q, -1)
        return remote(b_send, b_buf.at[origin], b_ssem.at[q], b_rsem.at[origin], far_mate(q))

    def c_copy(q):
        return remote(c_send.at[q], c_buf.at[q], c_ssem.at[q], c_rsem.at[q], far_mate(q))

    def d_copy(q):
        return remote(d_send, d_buf.at[q], d_ssem.at[q], d_rsem.at[q], mate(q))

    def over(first, last, action):
        for q in range(first, last):
            action(q)

    over(1, 8, lambda q: a_copy(q).start())
    up_copy = remote(halo_up, from_below, halo_sems.at[0], halo_sems.at[1], above)
    down_copy = remote(halo_down, from_above, halo_sems.at[2], halo_sems.at[3], below)
    up_copy.start()
    down_copy.start()

    find_points(order_v, inverse)
    up_copy.wait_recv()
    down_copy.wait_recv()

    def fill(e_ref, nodes, width, slot):
        for i in range(width):
            lower = jnp.where(me == 0, 0.0, unpack(from_below[slot + i]))
            upper = jnp.where(me == devices - 1, 0.0, unpack(from_above[slot + i]))
            e_ref[i] = e_rows(lower)
            e_ref[nodes + width + i] = e_rows(upper)

    fill(e_ord, 64, 1, 0)
    fill(e0, 64, 3, 1)
    fill(e1, 32, 3, 4)
    fill(e2, 16, 3, 7)

    def partners(g, picks, blocks, e_ref, shift, result):
        for half in range(2):
            lhs, w = [], []
            for s in range(3):
                rows = []
                for n in range(4):
                    node = 8 * g + 4 * half + n
                    rows.append(e_ref[node + shift(picks[s, node])])
                lhs.append(jnp.concatenate(rows, axis=0))
                w.append(prepare(blocks.at[s], g, half))
            result[2 * g + half] = pick_diagonal(times(lhs, w))

    def near_shift(pick):
        return pick + 1

    def far_shift(pick):
        return pick + (pick >> 1) * 3

    def near_part(first):
        each(
            4,
            NEAR_UNROLL,
            lambda g: partners(g + first, near_pick, near_v, e_ord, near_shift, near_f),
        )

    def half_of(w_ref, g, half):
        return w_ref[g, :, 128 * half : 128 * half + 128]

    def times_wide(lhs, w):
        return dot_nt(lhs, jnp.concatenate([w, w], axis=1))

    def z_to_e(groups):
        def step(g):
            for half in range(2):
                q = 2 * g + half
                moved = dot(jnp.concatenate(split(z_d[q]), axis=0), to_n[...])
                for i in range(2):
                    at = slice(128 * i, 128 * i + 128)
                    heads, rests = pair(moved[0:64, at]), pair(moved[64:, at])
                    for k in range(2):
                        z_e[4 * q + 2 * i + k] = jnp.concatenate(
                            [heads[k].astype(BF16), rests[k].astype(BF16)], axis=1
                        )

        each(groups, Z_UNROLL, step)

    def compose_two():
        identity = jnp.where(iota((64, 64), 0) == iota((64, 64), 1), 1.0, 0.0).astype(F32)
        lift_t = dot_nt(identity, lift, EXACT)
        start = e_rows(jnp.concatenate([lift_t, lift_t], axis=1))
        for q in range(4):
            z_d[q] = times_wide(start, half_of(w_tr, q // 2, q % 2))
        z_to_e(2)

    def compose(groups, w_ref):
        def step(g):
            for half in range(2):
                q = 2 * g + half
                first, second = z_e[2 * q], z_e[2 * q + 1]
                lhs = jnp.concatenate([first, first, second, second], axis=0)
                z_d[q] = pick_diagonal(times_wide(lhs, half_of(w_ref, g, half)), 64)

        each(groups, Z_UNROLL, step)
        z_to_e(groups)

    def compose_leaves():
        def step(g):
            for half in range(2):
                q = 2 * g + half
                lhs = z_e[pl.ds(4 * q, 4)].reshape(256, 256)
                head, rest = split(
                    pick_diagonal(times_wide(lhs, half_of(w_lb, g, half)), 64)
                )
                z_w[q] = jnp.concatenate([head, rest, head, rest], axis=0)

        each(8, Z_UNROLL, step)

    def to_e(values, quads):
        moved = dot(jnp.concatenate(split(values), axis=0), to_n[...])
        rows = 16 * quads
        for q in range(quads):
            for i in range(2):
                at = slice(128 * i, 128 * i + 128)
                heads = pair(moved[16 * q : 16 * q + 16, at])
                rests = pair(moved[rows + 16 * q : rows + 16 * q + 16, at])
                for k in range(2):
                    e_down[4 * q + 2 * i + k] = jnp.concatenate(
                        [heads[k].astype(BF16), rests[k].astype(BF16)], axis=1
                    )

    def descend(groups, w_ref, far):
        def step(g):
            for half in range(2):
                q = 2 * g + half
                first, second = e_down[2 * q], e_down[2 * q + 1]
                lhs = jnp.concatenate([first, first, second, second], axis=0)
                far[q] = far[q] + pick_diagonal(times([lhs], [half_of(w_ref, g, half)]))

        each(groups, DOWN_UNROLL, step)
        to_e(jnp.concatenate([far[q] for q in range(2 * groups)], axis=0), 2 * groups)

    def leaf_down(g):
        for half in range(2):
            q = 2 * g + half
            lhs = e_down[pl.ds(4 * q, 4)].reshape(64, 256)
            near_f[q] = near_f[q] + pick_diagonal(times([lhs], [half_of(w_lb, g, half)]))

    compose_two()
    compose(4, w_t2)

    over(1, 8, lambda q: a_copy(q).wait_recv())

    def total_of(buffer, slots):
        result = buffer[0]
        for q in range(1, slots):
            result = result + buffer[q]
        return result

    summed = total_of(a_buf, 8)
    b_send[...] = summed
    b_buf[group] = summed
    over(1, count, lambda q: b_copy(q).start())

    compose(8, w_t1)
    loads["near"].wait()
    near_part(0)
    near_part(4)
    loads["tb"].wait()
    w_top = split_rows([tb_v[pl.ds(n, 32, stride=4), :] for n in range(4)])

    over(1, count, lambda q: b_arrival(q).wait_recv())

    picked = []
    for b in range(4):
        picked.append(e_rows(unpack(b_buf[top_source[b]])))
    coupled = pick_diagonal(times([jnp.concatenate(picked, axis=0)], [w_top]))
    moved = dot(jnp.concatenate(split(coupled), axis=0), to_n[...])
    moved = moved[0:16] + moved[16:32]
    packed = []
    for i in range(2):
        packed += [pack(block) for block in pair(moved[:, 128 * i : 128 * i + 128])]
    for q in range(count):
        target = group_at(q)
        part = jnp.zeros((8, 128), F32)
        for b in range(4):
            part = part + jnp.where(jnp.full((8, 128), top_target[b]) == target, packed[b], 0.0)
        if q == 0:
            c_buf[0] = part
        else:
            c_send[q] = part
    over(1, count, lambda q: c_copy(q).start())

    compose_leaves()
    loads["fc"].wait()
    each(2, NEAR_UNROLL, lambda g: partners(g, pick_c, fc_v, e2, far_shift, far_c))
    loads["fb"].wait()
    each(4, NEAR_UNROLL, lambda g: partners(g, pick_b, fb_v, e1, far_shift, far_b))
    loads["fa"].wait()
    each(8, NEAR_UNROLL, lambda g: partners(g, pick_a, fa_v, e0, far_shift, far_a))

    over(1, count, lambda q: c_copy(q).wait_recv())
    summed = total_of(c_buf, count)
    d_send[...] = summed
    d_buf[0] = summed
    over(1, 8, lambda q: d_copy(q).start())

    to_e(jnp.concatenate([far_c[q] for q in range(4)], axis=0), 4)
    descend(4, w_t2, far_b)
    descend(8, w_t1, far_a)
    each(8, DOWN_UNROLL, leaf_down)

    over(1, 8, lambda q: d_copy(q).wait_recv())
    falling = e_rows(unpack(total_of(d_buf, 8)))
    for q in range(16):
        value = near_f[q] + dot(falling, z_w[q])
        for i in range(2):
            vals[2 * q + i] = value[:, 128 * i : 128 * i + 128]

    up_copy.wait_send()
    down_copy.wait_send()
    over(1, 8, lambda q: a_copy(q).wait_send())
    over(1, count, lambda q: b_copy(q).wait_send())
    over(1, count, lambda q: c_copy(q).wait_send())
    over(1, 8, lambda q: d_copy(q).wait_send())


def restore(vals, inverse, out):
    table = table_of([vals[t] for t in range(32)])
    for j in range(8):
        rows = [inverse[4 * j + i : 4 * j + i + 1, :] for i in range(4)]
        lanes = [inverse[4 * j + i + 32 : 4 * j + i + 33, :] for i in range(4)]
        out[:, 512 * j : 512 * j + 512] = lookup(
            table, jnp.concatenate(rows, axis=1), jnp.concatenate(lanes, axis=1)
        )


def lay_out(flat):
    lead, nodes = flat.shape[:-2], flat.shape[-2]
    n = min(nodes, 8)
    rows = jnp.swapaxes(flat.reshape(lead + (nodes // n, n, 32, 128)), -3, -2)
    return rows.reshape(lead + (nodes * 32, 128))


def body(devices, *args):
    smem, hbm = pl.BlockSpec(memory_space=pltpu.SMEM), pl.BlockSpec(memory_space=pl.ANY)
    vm, whole = pltpu.VMEM, pl.BlockSpec(memory_space=pltpu.VMEM)
    args = [lay_out(a) if i in (2, 4, 5, 6, 7, 9, 11, 13, 14, 17) else a for i, a in enumerate(args)]
    small = (3, 8, 10, 12, 15, 16)
    count = devices // 8
    big = [0, 1, 2, 4, 5, 6, 7, 9, 11, 13, 14, 17]
    dma = pltpu.SemaphoreType.DMA
    scratch = [vm(args[i].shape, args[i].dtype) for i in big]
    scratch += [
        vm((8, 256, 256), BF16),
        vm((8, 256, 256), BF16),
        vm((4, 256, 256), BF16),
        vm((2, 256, 256), BF16),
        vm((256, 256), BF16),
        vm((256, 256), BF16),
        vm((64, 256), BF16),
        vm((2, 16, 16, 256), BF16),
        vm((512, 256), BF16),
        vm((32, 16, 128), F32),
        vm((66, 16, 256), BF16),
        vm((70, 16, 256), BF16),
        vm((38, 16, 256), BF16),
        vm((22, 16, 256), BF16),
        vm((64, 16, 256), BF16),
        vm((16, 64, 256), F32),
        vm((64, 64, 256), BF16),
        vm((16, 256, 256), BF16),
        vm((16, 16, 256), F32),
        vm((16, 16, 256), F32),
        vm((8, 16, 256), F32),
        vm((4, 16, 256), F32),
        vm((10, 8, 128), F32),
        vm((10, 8, 128), F32),
        vm((10, 8, 128), F32),
        vm((10, 8, 128), F32),
        vm((8, 128), F32),
        vm((8, 8, 128), F32),
        vm((8, 128), F32),
        vm((count, 8, 128), F32),
        vm((count, 8, 128), F32),
        vm((count, 8, 128), F32),
        vm((8, 128), F32),
        vm((8, 8, 128), F32),
        dma((12,)),
        dma((4,)),
        dma((8,)),
        dma((8,)),
        dma((count,)),
        dma((count,)),
        dma((count,)),
        dma((count,)),
        dma((8,)),
        dma((8,)),
    ]
    vals, inverse = pl.pallas_call(
        functools.partial(kernel, devices),
        out_shape=(
            jax.ShapeDtypeStruct((32, 16, 128), F32),
            jax.ShapeDtypeStruct((64, 128), I32),
        ),
        in_specs=[smem if i in small else hbm for i in range(18)],
        out_specs=(whole, whole),
        scratch_shapes=scratch,
        compiler_params=pltpu.CompilerParams(
            collective_id=0, has_side_effects=True, vmem_limit_bytes=60 * 1024 * 1024
        ),
    )(*args)
    return pl.pallas_call(
        restore,
        out_shape=jax.ShapeDtypeStruct((16, 4096), F32),
        in_specs=[whole] * 2,
        out_specs=whole,
        compiler_params=pltpu.CompilerParams(vmem_limit_bytes=60 * 1024 * 1024),
    )(vals, inverse)


def solution(mesh):
    split_rows, split_columns = P("leaf", None), P(None, "leaf")
    split_middle = P(None, "leaf", None)
    in_specs = (
        split_columns,
        split_rows,
        split_rows,
        split_columns,
        split_middle,
        split_rows,
        split_rows,
        split_rows,
        split_columns,
        split_middle,
        split_columns,
        split_middle,
        split_columns,
        split_middle,
        split_middle,
        P("leaf"),
        P("leaf"),
        split_rows,
    )
    return jax.shard_map(
        functools.partial(body, mesh.shape["leaf"]),
        mesh=mesh,
        in_specs=in_specs,
        out_specs=split_columns,
        check_vma=False,
    )
```

```python
import functools

import jax
import jax.numpy as jnp
from jax import lax
from jax.experimental import pallas as pl
from jax.experimental.pallas import tpu as pltpu
from jax.sharding import PartitionSpec as P

F32, BF16, I32 = jnp.float32, jnp.bfloat16, jnp.int32
MESH = pl.DeviceIdType.MESH
EXACT = lax.Precision.HIGHEST
NEAR_UNROLL = 2
UP_UNROLL = 8
DOWN_UNROLL = 4
Z_UNROLL = 2


def iota(shape, dim):
    return lax.broadcasted_iota(I32, shape, dim)


def dot(a, b, precision=None):
    return lax.dot_general(
        a, b, (((1,), (0,)), ((), ())), precision=precision, preferred_element_type=F32
    )


def dot_nt(a, b, precision=None):
    return lax.dot_general(
        a, b, (((1,), (1,)), ((), ())), precision=precision, preferred_element_type=F32
    )


def split(x):
    head = x.astype(BF16)
    return head, (x - head.astype(F32)).astype(BF16)


def low_half(rows):
    return iota((rows, 128), 1) < 64


def swap(x):
    return pltpu.roll(x, 64, 1)


def prepare(ref, g, half):
    start = g * 256 + 4 * half
    return split_rows([ref[pl.ds(start + n, 32, stride=8), :] for n in range(4)])


def split_rows(matrices):
    a = jnp.concatenate(matrices, axis=0)
    head = a.astype(BF16)
    rest = (a - head.astype(F32)).astype(BF16)
    low = low_half(128)
    top = jnp.where(low, head, swap(rest))
    bottom = jnp.where(low, swap(head), rest)
    return jnp.concatenate([top, bottom], axis=0)


def pack(block):
    return jnp.where(low_half(8), block[0:8], block[8:16])


def unpack(packed):
    low, other = low_half(8), swap(packed)
    return jnp.concatenate(
        [jnp.where(low, packed, other), jnp.where(low, other, packed)], axis=0
    )


def pair(tile):
    low, other = low_half(tile.shape[0]), swap(tile)
    return jnp.where(low, tile, other), jnp.where(low, other, tile)


def e_rows(block):
    head, rest = split(block)
    return jnp.concatenate([head, rest], axis=1)


def pick_diagonal(wide, rows=16):
    lane_node = (iota((rows, 256), 1) >> 5) & 3
    result = wide[0:rows]
    for n in range(1, 4):
        result = jnp.where(lane_node == n, wide[rows * n : rows * n + rows], result)
    return result


def table_of(tiles):
    head, rest = split(jnp.concatenate(tiles, axis=0))
    return jnp.concatenate([head, rest], axis=1)


def lookup(table, tile_index, lane_index):
    width = lane_index.shape[1]
    hot = jnp.where(iota((128, width), 0) == lane_index, 1.0, 0.0).astype(BF16)
    found = dot(table, jnp.concatenate([hot, hot], axis=0))
    tile_index = jnp.broadcast_to(tile_index, (16, width))
    result = found[0:16]
    for s in range(1, 32):
        result = jnp.where(tile_index == s, found[16 * s : 16 * s + 16], result)
    return result


def find_points(order, inverse):
    def step(j, total):
        row = order[:, pl.ds(pl.multiple_of(j * 512, 512), 512)]
        lane = iota((1, 512), 1)
        n, p = lane >> 6, lane & 63
        parity, c = p & 1, p >> 1
        tile = (j * 4 + (n >> 2) * 2 + parity).astype(F32)
        place = ((n & 3) * 32 + c).astype(F32)
        chosen = iota((32, 512), 0) == (row >> 7)
        rows = jnp.concatenate(
            [jnp.where(chosen, tile, 0.0), jnp.where(chosen, place, 0.0)], axis=0
        ).astype(BF16)
        columns = jnp.where(iota((128, 512), 0) == (row & 127), 1.0, 0.0).astype(BF16)
        return total + dot_nt(rows, columns)

    inverse[...] = lax.fori_loop(0, 8, step, jnp.zeros((64, 128), F32), unroll=2).astype(I32)


def times(lhs_terms, w_terms):
    rows = lhs_terms[0].shape[0]
    heads = jnp.concatenate([lhs[:, :128] for lhs in lhs_terms], axis=1)
    rests = jnp.concatenate([lhs[:, 128:] for lhs in lhs_terms], axis=1)
    both = dot_nt(jnp.concatenate([heads, rests], axis=0), jnp.concatenate(w_terms, axis=1))
    return both[:rows] + both[rows:]


def kernel(
    devices,
    rhs_h, order_h, lb_h, near_pick, near_h, t1_h, t2_h, tr_h,
    pick_a, fa_h, pick_b, fb_h, pick_c, fc_h, tt_h, top_source, top_target, tb_h,
    vals, inverse,
    rhs_v, order_v, lb_v, near_v, t1_v, t2_v, tr_v, fa_v, fb_v, fc_v, tt_v, tb_v,
    w_lb, w_t1, w_t2, w_tr, to_d, to_n, diagonal, dmat, table, tiles,
    e_ord, e0, e1, e2, e_down, z_d, z_e, z_w, near_f, far_a, far_b, far_c,
    halo_up, halo_down, from_below, from_above,
    a_send, a_buf, b_send, b_buf, c_send, c_other, c_sum, c_buf, d_send, d_buf,
    load_sem, halo_sems, a_ssem, a_rsem, b_ssem, b_rsem, c_ssem, c_rsem, d_ssem, d_rsem,
):
    me = lax.axis_index("leaf")
    count = devices // 8
    inside, group = me & 7, me >> 3
    base = me - inside
    above, below = (me + 1) & (devices - 1), (me + devices - 1) & (devices - 1)
    deep = min(8, count)
    wide = count // deep
    line, depth = group // deep, group & (deep - 1)

    core, sibling = me & 1, me ^ 1
    share, turns = count // 2, max(deep // 2, 1)

    def offset(m, parity):
        dx = m // turns
        return dx, 2 * (m % turns) + ((parity ^ dx) & 1)

    def hops(m):
        dx, dz = offset(m, 0)
        return min(dx, wide - dx) + min(dz, deep - dz)

    order_of_turns = sorted(range(1, share), key=hops)[::-1]

    def group_at(m, parity):
        dx, dz = offset(m, parity)
        return ((line + dx) & (wide - 1)) * deep + ((depth + dz) & (deep - 1))

    def slot_of(node):
        dx = (line - (node >> (deep.bit_length() - 1))) & (wide - 1)
        dz = (depth - (node & (deep - 1))) & (deep - 1)
        return ((dx + dz) & 1) * share + dx * turns + (dz >> 1)

    def mate(q):
        return base + ((inside + q) & 7)

    def far_mate(q):
        return group_at(q, core) * 8 + inside

    def each_turn(action):
        for m in order_of_turns:
            action(m)
        pl.when(core == 1)(lambda: action(0))

    loads = {}

    def load(**pairs):
        for name, (src, dst) in pairs.items():
            loads[name] = pltpu.make_async_copy(src, dst, load_sem.at[len(loads)])
            loads[name].start()

    load(order=(order_h, order_v), rhs=(rhs_h, rhs_v), lb=(lb_h, lb_v), t1=(t1_h, t1_v))
    load(t2=(t2_h, t2_v), tr=(tr_h, tr_v), tt=(tt_h, tt_v))

    barrier = pltpu.get_barrier_semaphore()

    def greet(device):
        pl.semaphore_signal(barrier, inc=1, device_id=(device,), device_id_type=MESH)

    greet(above)
    greet(below)

    @pl.loop(1, 8)
    def _(q):
        greet(mate(q))

    each_turn(lambda m: greet(far_mate(m)))

    rows, lanes = iota((256, 256), 0), iota((256, 256), 1)

    def natural(place):
        return ((place >> 5) & 3) * 64 + (place & 31) * 2 + (place >> 7)

    to_d[...] = jnp.where(rows == natural(lanes), 1.0, 0.0).astype(BF16)
    to_n[...] = jnp.where(lanes == natural(rows), 1.0, 0.0).astype(BF16)
    diagonal[...] = jnp.where(
        ((iota((64, 256), 1) >> 5) & 3) == (iota((64, 256), 0) >> 4), 1.0, 0.0
    ).astype(BF16)

    loads["rhs"].wait()
    table[...] = table_of([rhs_v[:, 128 * t : 128 * t + 128] for t in range(32)])
    loads["order"].wait()
    split_next = [
        (name, ref, w, g)
        for name, ref, w, groups in (
            ("lb", lb_v, w_lb, 8), ("t1", t1_v, w_t1, 8), ("t2", t2_v, w_t2, 4), ("tr", tr_v, w_tr, 2)
        )
        for g in range(groups)
    ]

    def split_one():
        name, ref, w, g = split_next.pop(0)
        if g == 0:
            loads[name].wait()
        for half in range(2):
            w[g, :, 128 * half : 128 * half + 128] = prepare(ref, g, half)

    for j in range(8):
        row = order_v[:, 512 * j : 512 * j + 512]
        found = lookup(table[...], row >> 7, row & 127)
        for i in range(4):
            tile = found[:, 128 * i : 128 * i + 128]
            tiles[4 * j + i] = tile
            for k, block in enumerate(pair(tile)):
                e_ord[8 * j + 2 * i + k + 1] = e_rows(block)
        for _ in range(min(j + 1, 3)):
            split_one()
    while split_next:
        split_one()
    load(near=(near_h, near_v), fa=(fa_h, fa_v), fb=(fb_h, fb_v), fc=(fc_h, fc_v), tb=(tb_h, tb_v))

    loads["tt"].wait()
    sort = jnp.where(
        iota((64, 64), 0) == (iota((64, 64), 1) & 31) * 2 + (iota((64, 64), 1) >> 5), 1.0, 0.0
    ).astype(F32)

    def top_matrix(j):
        rows = tt_v[j]
        return dot(sort, jnp.concatenate([rows[:, :64], rows[:, 64:]], axis=0), EXACT)

    lift = dot(top_matrix(0), dot(top_matrix(1), top_matrix(2), EXACT), EXACT)
    lift_wide = jnp.concatenate([lift, lift], axis=1)

    def spread_rows(groups):
        quads = 2 * groups
        x = jnp.concatenate(
            [jnp.concatenate([tiles[2 * q], tiles[2 * q + 1]], axis=1) for q in range(quads)], axis=0
        )
        moved = dot(jnp.concatenate(split(x), axis=0), to_d[...]).astype(BF16)
        dmat[0, 0:quads] = moved[0 : 16 * quads].reshape(quads, 16, 256)
        dmat[1, 0:quads] = moved[16 * quads :].reshape(quads, 16, 256)

    def up_group(g, w):
        mask = diagonal[...]
        lhs = jnp.concatenate(
            [
                jnp.concatenate([dmat[part, 2 * g + half]] * 4, axis=0) * mask
                for half in range(2)
                for part in range(2)
            ],
            axis=0,
        )
        product = dot(lhs, w)
        results = []
        for half in range(2):
            at = slice(128 * half, 128 * half + 128)
            both = product[128 * half : 128 * half + 64, at] + product[128 * half + 64 : 128 * half + 128, at]
            results.append(both + swap(both))
        return jnp.concatenate(results, axis=0)

    def each(groups, unroll, step):
        def body(g, carry):
            step(g)
            return carry

        lax.fori_loop(0, groups, body, 0, unroll=min(unroll, groups))

    halo_down[0] = pack(pair(tiles[0])[0])
    halo_up[0] = pack(pair(tiles[31])[1])

    spread_rows(8)

    def leaf_up(g):
        r = up_group(g, w_lb[g])
        e0[pl.ds(8 * g + 3, 8)] = e_rows(r).reshape(8, 16, 256)
        for i in range(4):
            tiles[4 * g + i] = jnp.where(
                low_half(16), r[32 * i : 32 * i + 16], r[32 * i + 16 : 32 * i + 32]
            )

    each(8, UP_UNROLL, leaf_up)

    def keep_ends(slot, nodes):
        for i in range(3):
            first, last = tiles[i // 2], tiles[(nodes - 3 + i) // 2]
            halo_down[slot + i] = pack(pair(first)[i % 2])
            halo_up[slot + i] = pack(pair(last)[(nodes - 3 + i) % 2])

    keep_ends(1, 64)

    def climb(groups, w_ref, e_ref):
        spread_rows(groups)

        def step(g):
            r = up_group(g, w_ref[g])
            parents = [r[32 * i : 32 * i + 16] + r[32 * i + 16 : 32 * i + 32] for i in range(4)]
            for i in range(2):
                tiles[2 * g + i] = jnp.where(low_half(16), parents[2 * i], parents[2 * i + 1])
            for i in range(4):
                e_ref[4 * g + 3 + i] = e_rows(parents[i])

        each(groups, UP_UNROLL, step)

    climb(8, w_t1, e1)
    keep_ends(4, 32)
    climb(4, w_t2, e2)
    keep_ends(7, 16)

    spread_rows(2)
    rooted = jnp.zeros((16, 128), F32)
    for g in range(2):
        r = up_group(g, w_tr[g])
        for n in range(8):
            rooted = rooted + r[16 * n : 16 * n + 16]
    offered = pack(dot(rooted[:, :64], lift_wide, EXACT))
    a_send[...] = offered
    a_buf[0] = offered

    pl.semaphore_wait(barrier, 2 + 7 + share - 1 + core)

    def remote(src, dst, send, receive, device):
        return pltpu.make_async_remote_copy(
            src_ref=src, dst_ref=dst, send_sem=send, recv_sem=receive,
            device_id=(device,), device_id_type=MESH,
        )

    def a_copy(q):
        return remote(a_send, a_buf.at[q], a_ssem.at[q], a_rsem.at[q], mate(q))

    def b_copy(m):
        at = core * share + m
        return remote(b_send, b_buf.at[at], b_ssem.at[m], b_rsem.at[m], far_mate(m))

    half_here = pl.ds(core * share, share)
    half_there = pl.ds((1 - core) * share, share)
    b_half = remote(b_buf.at[half_here], b_buf.at[half_here], halo_sems.at[4], halo_sems.at[5], sibling)
    c_half = remote(c_send.at[half_there], c_other, halo_sems.at[6], halo_sems.at[7], sibling)

    def c_copy(m):
        return remote(c_sum.at[m], c_buf.at[m], c_ssem.at[m], c_rsem.at[m], far_mate(m))

    def d_copy(q):
        return remote(d_send, d_buf.at[q], d_ssem.at[q], d_rsem.at[q], mate(q))

    def over(first, last, action):
        for q in range(first, last):
            action(q)

    over(1, 8, lambda q: a_copy(q).start())
    up_copy = remote(halo_up, from_below, halo_sems.at[0], halo_sems.at[1], above)
    down_copy = remote(halo_down, from_above, halo_sems.at[2], halo_sems.at[3], below)
    up_copy.start()
    down_copy.start()

    find_points(order_v, inverse)
    up_copy.wait_recv()
    down_copy.wait_recv()

    def fill(e_ref, nodes, width, slot):
        for i in range(width):
            lower = jnp.where(me == 0, 0.0, unpack(from_below[slot + i]))
            upper = jnp.where(me == devices - 1, 0.0, unpack(from_above[slot + i]))
            e_ref[i] = e_rows(lower)
            e_ref[nodes + width + i] = e_rows(upper)

    fill(e_ord, 64, 1, 0)
    fill(e0, 64, 3, 1)
    fill(e1, 32, 3, 4)
    fill(e2, 16, 3, 7)

    def partners(g, picks, blocks, e_ref, shift, result):
        for half in range(2):
            lhs, w = [], []
            for s in range(3):
                rows = []
                for n in range(4):
                    node = 8 * g + 4 * half + n
                    rows.append(e_ref[node + shift(picks[s, node])])
                lhs.append(jnp.concatenate(rows, axis=0))
                w.append(prepare(blocks.at[s], g, half))
            result[2 * g + half] = pick_diagonal(times(lhs, w))

    def near_shift(pick):
        return pick + 1

    def far_shift(pick):
        return pick + (pick >> 1) * 3

    def near_part(first):
        each(
            4,
            NEAR_UNROLL,
            lambda g: partners(g + first, near_pick, near_v, e_ord, near_shift, near_f),
        )

    def half_of(w_ref, g, half):
        return w_ref[g, :, 128 * half : 128 * half + 128]

    def times_wide(lhs, w):
        return dot_nt(lhs, jnp.concatenate([w, w], axis=1))

    def z_to_e(groups):
        def step(g):
            for half in range(2):
                q = 2 * g + half
                moved = dot(jnp.concatenate(split(z_d[q]), axis=0), to_n[...])
                for i in range(2):
                    at = slice(128 * i, 128 * i + 128)
                    heads, rests = pair(moved[0:64, at]), pair(moved[64:, at])
                    for k in range(2):
                        z_e[4 * q + 2 * i + k] = jnp.concatenate(
                            [heads[k].astype(BF16), rests[k].astype(BF16)], axis=1
                        )

        each(groups, Z_UNROLL, step)

    def compose_two():
        identity = jnp.where(iota((64, 64), 0) == iota((64, 64), 1), 1.0, 0.0).astype(F32)
        lift_t = dot_nt(identity, lift, EXACT)
        start = e_rows(jnp.concatenate([lift_t, lift_t], axis=1))
        for q in range(4):
            z_d[q] = times_wide(start, half_of(w_tr, q // 2, q % 2))
        z_to_e(2)

    def compose(groups, w_ref):
        def step(g):
            for half in range(2):
                q = 2 * g + half
                first, second = z_e[2 * q], z_e[2 * q + 1]
                lhs = jnp.concatenate([first, first, second, second], axis=0)
                z_d[q] = pick_diagonal(times_wide(lhs, half_of(w_ref, g, half)), 64)

        each(groups, Z_UNROLL, step)
        z_to_e(groups)

    def compose_leaves():
        def step(g):
            for half in range(2):
                q = 2 * g + half
                lhs = z_e[pl.ds(4 * q, 4)].reshape(256, 256)
                head, rest = split(
                    pick_diagonal(times_wide(lhs, half_of(w_lb, g, half)), 64)
                )
                z_w[q] = jnp.concatenate([head, rest, head, rest], axis=0)

        each(8, Z_UNROLL, step)

    def to_e(values, quads):
        moved = dot(jnp.concatenate(split(values), axis=0), to_n[...])
        rows = 16 * quads
        for q in range(quads):
            for i in range(2):
                at = slice(128 * i, 128 * i + 128)
                heads = pair(moved[16 * q : 16 * q + 16, at])
                rests = pair(moved[rows + 16 * q : rows + 16 * q + 16, at])
                for k in range(2):
                    e_down[4 * q + 2 * i + k] = jnp.concatenate(
                        [heads[k].astype(BF16), rests[k].astype(BF16)], axis=1
                    )

    def descend(groups, w_ref, far):
        def step(g):
            for half in range(2):
                q = 2 * g + half
                first, second = e_down[2 * q], e_down[2 * q + 1]
                lhs = jnp.concatenate([first, first, second, second], axis=0)
                far[q] = far[q] + pick_diagonal(times([lhs], [half_of(w_ref, g, half)]))

        each(groups, DOWN_UNROLL, step)
        to_e(jnp.concatenate([far[q] for q in range(2 * groups)], axis=0), 2 * groups)

    def leaf_down(g):
        for half in range(2):
            q = 2 * g + half
            lhs = e_down[pl.ds(4 * q, 4)].reshape(64, 256)
            near_f[q] = near_f[q] + pick_diagonal(times([lhs], [half_of(w_lb, g, half)]))

    compose_two()
    compose(4, w_t2)

    over(1, 8, lambda q: a_copy(q).wait_recv())

    def total_of(buffer, slots):
        result = buffer[0]
        for q in range(1, slots):
            result = result + buffer[q]
        return result

    summed = total_of(a_buf, 8)
    b_send[...] = summed

    @pl.when(core == 0)
    def _():
        b_buf[0] = summed

    each_turn(lambda m: b_copy(m).start())

    compose(8, w_t1)
    loads["near"].wait()
    near_part(0)
    near_part(4)
    loads["tb"].wait()
    w_top = split_rows([tb_v[pl.ds(n, 32, stride=4), :] for n in range(4)])

    each_turn(lambda m: b_copy(m).wait_recv())
    b_half.start()
    b_half.wait_recv()

    picked = []
    for b in range(4):
        picked.append(e_rows(unpack(b_buf[slot_of(top_source[b])])))
    coupled = pick_diagonal(times([jnp.concatenate(picked, axis=0)], [w_top]))
    moved = dot(jnp.concatenate(split(coupled), axis=0), to_n[...])
    moved = moved[0:16] + moved[16:32]
    packed = []
    for i in range(2):
        packed += [pack(block) for block in pair(moved[:, 128 * i : 128 * i + 128])]
    for parity in range(2):
        for m in range(share):
            target = group_at(m, parity)
            part = jnp.zeros((8, 128), F32)
            for b in range(4):
                part = part + jnp.where(jnp.full((8, 128), top_target[b]) == target, packed[b], 0.0)
            c_send[parity * share + m] = part
    c_half.start()
    c_half.wait_recv()
    for m in range(share):
        c_sum[m] = c_send[core * share + m] + c_other[m]

    @pl.when(core == 0)
    def _():
        c_buf[0] = c_sum[0]

    each_turn(lambda m: c_copy(m).start())

    compose_leaves()
    loads["fc"].wait()
    each(2, NEAR_UNROLL, lambda g: partners(g, pick_c, fc_v, e2, far_shift, far_c))
    loads["fb"].wait()
    each(4, NEAR_UNROLL, lambda g: partners(g, pick_b, fb_v, e1, far_shift, far_b))
    loads["fa"].wait()
    each(8, NEAR_UNROLL, lambda g: partners(g, pick_a, fa_v, e0, far_shift, far_a))

    each_turn(lambda m: c_copy(m).wait_recv())
    summed = total_of(c_buf, share)
    d_send[...] = summed
    d_buf[0] = summed
    over(1, 8, lambda q: d_copy(q).start())

    to_e(jnp.concatenate([far_c[q] for q in range(4)], axis=0), 4)
    descend(4, w_t2, far_b)
    descend(8, w_t1, far_a)
    each(8, DOWN_UNROLL, leaf_down)

    over(1, 8, lambda q: d_copy(q).wait_recv())
    falling = e_rows(unpack(total_of(d_buf, 8)))
    for q in range(16):
        value = near_f[q] + dot(falling, z_w[q])
        for i in range(2):
            vals[2 * q + i] = value[:, 128 * i : 128 * i + 128]

    up_copy.wait_send()
    down_copy.wait_send()
    over(1, 8, lambda q: a_copy(q).wait_send())
    b_half.wait_send()
    c_half.wait_send()
    each_turn(lambda m: b_copy(m).wait_send())
    each_turn(lambda m: c_copy(m).wait_send())
    over(1, 8, lambda q: d_copy(q).wait_send())


def restore(vals, inverse, out):
    table = table_of([vals[t] for t in range(32)])
    for j in range(8):
        rows = [inverse[4 * j + i : 4 * j + i + 1, :] for i in range(4)]
        lanes = [inverse[4 * j + i + 32 : 4 * j + i + 33, :] for i in range(4)]
        out[:, 512 * j : 512 * j + 512] = lookup(
            table, jnp.concatenate(rows, axis=1), jnp.concatenate(lanes, axis=1)
        )


def lay_out(flat):
    lead, nodes = flat.shape[:-2], flat.shape[-2]
    n = min(nodes, 8)
    rows = jnp.swapaxes(flat.reshape(lead + (nodes // n, n, 32, 128)), -3, -2)
    return rows.reshape(lead + (nodes * 32, 128))


def body(devices, *args):
    smem, hbm = pl.BlockSpec(memory_space=pltpu.SMEM), pl.BlockSpec(memory_space=pl.ANY)
    vm, whole = pltpu.VMEM, pl.BlockSpec(memory_space=pltpu.VMEM)
    args = [lay_out(a) if i in (2, 4, 5, 6, 7, 9, 11, 13, 14, 17) else a for i, a in enumerate(args)]
    small = (3, 8, 10, 12, 15, 16)
    count = devices // 8
    big = [0, 1, 2, 4, 5, 6, 7, 9, 11, 13, 14, 17]
    dma = pltpu.SemaphoreType.DMA
    scratch = [vm(args[i].shape, args[i].dtype) for i in big]
    scratch += [
        vm((8, 256, 256), BF16),
        vm((8, 256, 256), BF16),
        vm((4, 256, 256), BF16),
        vm((2, 256, 256), BF16),
        vm((256, 256), BF16),
        vm((256, 256), BF16),
        vm((64, 256), BF16),
        vm((2, 16, 16, 256), BF16),
        vm((512, 256), BF16),
        vm((32, 16, 128), F32),
        vm((66, 16, 256), BF16),
        vm((70, 16, 256), BF16),
        vm((38, 16, 256), BF16),
        vm((22, 16, 256), BF16),
        vm((64, 16, 256), BF16),
        vm((16, 64, 256), F32),
        vm((64, 64, 256), BF16),
        vm((16, 256, 256), BF16),
        vm((16, 16, 256), F32),
        vm((16, 16, 256), F32),
        vm((8, 16, 256), F32),
        vm((4, 16, 256), F32),
        vm((10, 8, 128), F32),
        vm((10, 8, 128), F32),
        vm((10, 8, 128), F32),
        vm((10, 8, 128), F32),
        vm((8, 128), F32),
        vm((8, 8, 128), F32),
        vm((8, 128), F32),
        vm((count, 8, 128), F32),
        vm((count, 8, 128), F32),
        vm((count // 2, 8, 128), F32),
        vm((count // 2, 8, 128), F32),
        vm((count // 2, 8, 128), F32),
        vm((8, 128), F32),
        vm((8, 8, 128), F32),
        dma((12,)),
        dma((8,)),
        dma((8,)),
        dma((8,)),
        dma((count // 2,)),
        dma((count // 2,)),
        dma((count // 2,)),
        dma((count // 2,)),
        dma((8,)),
        dma((8,)),
    ]
    vals, inverse = pl.pallas_call(
        functools.partial(kernel, devices),
        out_shape=(
            jax.ShapeDtypeStruct((32, 16, 128), F32),
            jax.ShapeDtypeStruct((64, 128), I32),
        ),
        in_specs=[smem if i in small else hbm for i in range(18)],
        out_specs=(whole, whole),
        scratch_shapes=scratch,
        compiler_params=pltpu.CompilerParams(
            collective_id=0, has_side_effects=True, vmem_limit_bytes=60 * 1024 * 1024
        ),
    )(*args)
    return pl.pallas_call(
        restore,
        out_shape=jax.ShapeDtypeStruct((16, 4096), F32),
        in_specs=[whole] * 2,
        out_specs=whole,
        compiler_params=pltpu.CompilerParams(vmem_limit_bytes=60 * 1024 * 1024),
    )(vals, inverse)


def solution(mesh):
    split_rows, split_columns = P("leaf", None), P(None, "leaf")
    split_middle = P(None, "leaf", None)
    in_specs = (
        split_columns,
        split_rows,
        split_rows,
        split_columns,
        split_middle,
        split_rows,
        split_rows,
        split_rows,
        split_columns,
        split_middle,
        split_columns,
        split_middle,
        split_columns,
        split_middle,
        split_middle,
        P("leaf"),
        P("leaf"),
        split_rows,
    )
    return jax.shard_map(
        functools.partial(body, mesh.shape["leaf"]),
        mesh=mesh,
        in_specs=in_specs,
        out_specs=split_columns,
        check_vma=False,
    )
```

```python
import functools

import jax
import jax.numpy as jnp
from jax import lax
from jax.experimental import pallas as pl
from jax.experimental.pallas import tpu as pltpu
from jax.sharding import PartitionSpec as P

F32, BF16, I32 = jnp.float32, jnp.bfloat16, jnp.int32
MESH = pl.DeviceIdType.MESH
EXACT = lax.Precision.HIGHEST
NEAR_UNROLL = 2
UP_UNROLL = 8
DOWN_UNROLL = 4
Z_UNROLL = 2


def iota(shape, dim):
    return lax.broadcasted_iota(I32, shape, dim)


def dot(a, b, precision=None):
    return lax.dot_general(
        a, b, (((1,), (0,)), ((), ())), precision=precision, preferred_element_type=F32
    )


def dot_nt(a, b, precision=None):
    return lax.dot_general(
        a, b, (((1,), (1,)), ((), ())), precision=precision, preferred_element_type=F32
    )


def split(x):
    head = x.astype(BF16)
    return head, (x - head.astype(F32)).astype(BF16)


def low_half(rows):
    return iota((rows, 128), 1) < 64


def swap(x):
    return pltpu.roll(x, 64, 1)


def prepare(ref, g, half):
    start = g * 256 + 4 * half
    return split_rows([ref[pl.ds(start + n, 32, stride=8), :] for n in range(4)])


def split_rows(matrices):
    a = jnp.concatenate(matrices, axis=0)
    head = a.astype(BF16)
    rest = (a - head.astype(F32)).astype(BF16)
    low = low_half(128)
    top = jnp.where(low, head, swap(rest))
    bottom = jnp.where(low, swap(head), rest)
    return jnp.concatenate([top, bottom], axis=0)


def pack(block):
    return jnp.where(low_half(8), block[0:8], block[8:16])


def unpack(packed):
    low, other = low_half(8), swap(packed)
    return jnp.concatenate(
        [jnp.where(low, packed, other), jnp.where(low, other, packed)], axis=0
    )


def pair(tile):
    low, other = low_half(tile.shape[0]), swap(tile)
    return jnp.where(low, tile, other), jnp.where(low, other, tile)


def e_rows(block):
    head, rest = split(block)
    return jnp.concatenate([head, rest], axis=1)


def pick_diagonal(wide, rows=16):
    lane_node = (iota((rows, 256), 1) >> 5) & 3
    result = wide[0:rows]
    for n in range(1, 4):
        result = jnp.where(lane_node == n, wide[rows * n : rows * n + rows], result)
    return result


def table_of(tiles):
    head, rest = split(jnp.concatenate(tiles, axis=0))
    return jnp.concatenate([head, rest], axis=1)


def lookup(table, tile_index, lane_index):
    width = lane_index.shape[1]
    hot = jnp.where(iota((128, width), 0) == lane_index, 1.0, 0.0).astype(BF16)
    found = dot(table, jnp.concatenate([hot, hot], axis=0))
    tile_index = jnp.broadcast_to(tile_index, (16, width))
    result = found[0:16]
    for s in range(1, 32):
        result = jnp.where(tile_index == s, found[16 * s : 16 * s + 16], result)
    return result


def find_points(order, inverse):
    def step(j, total):
        row = order[:, pl.ds(pl.multiple_of(j * 512, 512), 512)]
        lane = iota((1, 512), 1)
        n, p = lane >> 6, lane & 63
        parity, c = p & 1, p >> 1
        tile = (j * 4 + (n >> 2) * 2 + parity).astype(F32)
        place = ((n & 3) * 32 + c).astype(F32)
        chosen = iota((32, 512), 0) == (row >> 7)
        rows = jnp.concatenate(
            [jnp.where(chosen, tile, 0.0), jnp.where(chosen, place, 0.0)], axis=0
        ).astype(BF16)
        columns = jnp.where(iota((128, 512), 0) == (row & 127), 1.0, 0.0).astype(BF16)
        return total + dot_nt(rows, columns)

    inverse[...] = lax.fori_loop(0, 8, step, jnp.zeros((64, 128), F32), unroll=2).astype(I32)


def times(lhs_terms, w_terms):
    rows = lhs_terms[0].shape[0]
    heads = jnp.concatenate([lhs[:, :128] for lhs in lhs_terms], axis=1)
    rests = jnp.concatenate([lhs[:, 128:] for lhs in lhs_terms], axis=1)
    both = dot_nt(jnp.concatenate([heads, rests], axis=0), jnp.concatenate(w_terms, axis=1))
    return both[:rows] + both[rows:]


def kernel(
    devices,
    rhs_h, order_h, lb_h, near_pick, near_h, t1_h, t2_h, tr_h,
    pick_a, fa_h, pick_b, fb_h, pick_c, fc_h, tt_h, top_source, top_target, tb_h,
    vals, inverse,
    rhs_v, order_v, lb_v, near_v, t1_v, t2_v, tr_v, fa_v, fb_v, fc_v, tt_v, tb_v,
    w_lb, w_t1, w_t2, w_tr, to_d, to_n, diagonal, dmat, table, tiles,
    e_ord, e0, e1, e2, e_down, z_d, z_e, z_w, near_f, far_a, far_b, far_c,
    halo_up, halo_down, from_below, from_above,
    a_send, a_buf, b_send, b_buf, c_send, c_buf, d_send, d_buf,
    load_sem, halo_sems, a_ssem, a_rsem, b_ssem, b_rsem, c_ssem, c_rsem, d_ssem, d_rsem,
):
    me = lax.axis_index("leaf")
    count = devices // 8
    inside, group = me & 7, me >> 3
    base = me - inside
    above, below = (me + 1) & (devices - 1), (me + devices - 1) & (devices - 1)
    deep = min(8, count)
    wide = count // deep
    line, depth = group // deep, group & (deep - 1)

    def hops(offset):
        dx, dz = offset
        return min(dx, wide - dx) + min(dz, deep - dz)

    offsets = sorted(((dx, dz) for dx in range(wide) for dz in range(deep)), key=hops)[::-1]
    offsets = [(0, 0)] + offsets[:-1]

    def group_at(q, sign=1):
        dx, dz = offsets[q]
        dx, dz = (dx, dz) if sign > 0 else (wide - dx, deep - dz)
        return ((line + dx) & (wide - 1)) * deep + ((depth + dz) & (deep - 1))

    def mate(q):
        return base + ((inside + q) & 7)

    def far_mate(q):
        return group_at(q) * 8 + inside

    loads = {}

    def load(**pairs):
        for name, (src, dst) in pairs.items():
            loads[name] = pltpu.make_async_copy(src, dst, load_sem.at[len(loads)])
            loads[name].start()

    load(order=(order_h, order_v), rhs=(rhs_h, rhs_v), lb=(lb_h, lb_v), t1=(t1_h, t1_v))
    load(t2=(t2_h, t2_v), tr=(tr_h, tr_v), tt=(tt_h, tt_v))

    barrier = pltpu.get_barrier_semaphore()

    def greet(device):
        pl.semaphore_signal(barrier, inc=1, device_id=(device,), device_id_type=MESH)

    greet(above)
    greet(below)

    @pl.loop(1, 8)
    def _(q):
        greet(mate(q))

    for q in range(1, count):
        greet(far_mate(q))

    rows, lanes = iota((256, 256), 0), iota((256, 256), 1)

    def natural(place):
        return ((place >> 5) & 3) * 64 + (place & 31) * 2 + (place >> 7)

    to_d[...] = jnp.where(rows == natural(lanes), 1.0, 0.0).astype(BF16)
    to_n[...] = jnp.where(lanes == natural(rows), 1.0, 0.0).astype(BF16)
    diagonal[...] = jnp.where(
        ((iota((64, 256), 1) >> 5) & 3) == (iota((64, 256), 0) >> 4), 1.0, 0.0
    ).astype(BF16)

    loads["rhs"].wait()
    table[...] = table_of([rhs_v[:, 128 * t : 128 * t + 128] for t in range(32)])
    loads["order"].wait()
    split_next = [
        (name, ref, w, g)
        for name, ref, w, groups in (
            ("lb", lb_v, w_lb, 8), ("t1", t1_v, w_t1, 8), ("t2", t2_v, w_t2, 4), ("tr", tr_v, w_tr, 2)
        )
        for g in range(groups)
    ]

    def split_one():
        name, ref, w, g = split_next.pop(0)
        if g == 0:
            loads[name].wait()
        for half in range(2):
            w[g, :, 128 * half : 128 * half + 128] = prepare(ref, g, half)

    for j in range(8):
        row = order_v[:, 512 * j : 512 * j + 512]
        found = lookup(table[...], row >> 7, row & 127)
        for i in range(4):
            tile = found[:, 128 * i : 128 * i + 128]
            tiles[4 * j + i] = tile
            for k, block in enumerate(pair(tile)):
                e_ord[8 * j + 2 * i + k + 1] = e_rows(block)
        for _ in range(min(j + 1, 3)):
            split_one()
    while split_next:
        split_one()
    load(near=(near_h, near_v), fa=(fa_h, fa_v), fb=(fb_h, fb_v), fc=(fc_h, fc_v), tb=(tb_h, tb_v))

    loads["tt"].wait()
    sort = jnp.where(
        iota((64, 64), 0) == (iota((64, 64), 1) & 31) * 2 + (iota((64, 64), 1) >> 5), 1.0, 0.0
    ).astype(F32)

    def top_matrix(j):
        rows = tt_v[j]
        return dot(sort, jnp.concatenate([rows[:, :64], rows[:, 64:]], axis=0), EXACT)

    lift = dot(top_matrix(0), dot(top_matrix(1), top_matrix(2), EXACT), EXACT)
    lift_wide = jnp.concatenate([lift, lift], axis=1)

    def spread_rows(groups):
        quads = 2 * groups
        x = jnp.concatenate(
            [jnp.concatenate([tiles[2 * q], tiles[2 * q + 1]], axis=1) for q in range(quads)], axis=0
        )
        moved = dot(jnp.concatenate(split(x), axis=0), to_d[...]).astype(BF16)
        dmat[0, 0:quads] = moved[0 : 16 * quads].reshape(quads, 16, 256)
        dmat[1, 0:quads] = moved[16 * quads :].reshape(quads, 16, 256)

    def up_group(g, w):
        mask = diagonal[...]
        lhs = jnp.concatenate(
            [
                jnp.concatenate([dmat[part, 2 * g + half]] * 4, axis=0) * mask
                for half in range(2)
                for part in range(2)
            ],
            axis=0,
        )
        product = dot(lhs, w)
        results = []
        for half in range(2):
            at = slice(128 * half, 128 * half + 128)
            both = product[128 * half : 128 * half + 64, at] + product[128 * half + 64 : 128 * half + 128, at]
            results.append(both + swap(both))
        return jnp.concatenate(results, axis=0)

    def each(groups, unroll, step):
        def body(g, carry):
            step(g)
            return carry

        lax.fori_loop(0, groups, body, 0, unroll=min(unroll, groups))

    halo_down[0] = pack(pair(tiles[0])[0])
    halo_up[0] = pack(pair(tiles[31])[1])

    spread_rows(8)

    def leaf_up(g):
        r = up_group(g, w_lb[g])
        e0[pl.ds(8 * g + 3, 8)] = e_rows(r).reshape(8, 16, 256)
        for i in range(4):
            tiles[4 * g + i] = jnp.where(
                low_half(16), r[32 * i : 32 * i + 16], r[32 * i + 16 : 32 * i + 32]
            )

    each(8, UP_UNROLL, leaf_up)

    def keep_ends(slot, nodes):
        for i in range(3):
            first, last = tiles[i // 2], tiles[(nodes - 3 + i) // 2]
            halo_down[slot + i] = pack(pair(first)[i % 2])
            halo_up[slot + i] = pack(pair(last)[(nodes - 3 + i) % 2])

    keep_ends(1, 64)

    def climb(groups, w_ref, e_ref):
        spread_rows(groups)

        def step(g):
            r = up_group(g, w_ref[g])
            parents = [r[32 * i : 32 * i + 16] + r[32 * i + 16 : 32 * i + 32] for i in range(4)]
            for i in range(2):
                tiles[2 * g + i] = jnp.where(low_half(16), parents[2 * i], parents[2 * i + 1])
            for i in range(4):
                e_ref[4 * g + 3 + i] = e_rows(parents[i])

        each(groups, UP_UNROLL, step)

    climb(8, w_t1, e1)
    keep_ends(4, 32)
    climb(4, w_t2, e2)
    keep_ends(7, 16)

    spread_rows(2)
    rooted = jnp.zeros((16, 128), F32)
    for g in range(2):
        r = up_group(g, w_tr[g])
        for n in range(8):
            rooted = rooted + r[16 * n : 16 * n + 16]
    offered = pack(dot(rooted[:, :64], lift_wide, EXACT))
    a_send[...] = offered
    a_buf[0] = offered

    pl.semaphore_wait(barrier, 2 + 7 + count - 1)

    def remote(src, dst, send, receive, device):
        return pltpu.make_async_remote_copy(
            src_ref=src, dst_ref=dst, send_sem=send, recv_sem=receive,
            device_id=(device,), device_id_type=MESH,
        )

    def a_copy(q):
        return remote(a_send, a_buf.at[q], a_ssem.at[q], a_rsem.at[q], mate(q))

    def b_copy(q):
        return remote(b_send, b_buf.at[group], b_ssem.at[q], b_rsem.at[group], far_mate(q))

    def b_arrival(q):
        origin = group_at(q, -1)
        return remote(b_send, b_buf.at[origin], b_ssem.at[q], b_rsem.at[origin], far_mate(q))

    def c_copy(q):
        return remote(c_send.at[q], c_buf.at[q], c_ssem.at[q], c_rsem.at[q], far_mate(q))

    def d_copy(q):
        return remote(d_send, d_buf.at[q], d_ssem.at[q], d_rsem.at[q], mate(q))

    def over(first, last, action):
        for q in range(first, last):
            action(q)

    over(1, 8, lambda q: a_copy(q).start())
    up_copy = remote(halo_up, from_below, halo_sems.at[0], halo_sems.at[1], above)
    down_copy = remote(halo_down, from_above, halo_sems.at[2], halo_sems.at[3], below)
    up_copy.start()
    down_copy.start()

    find_points(order_v, inverse)
    up_copy.wait_recv()
    down_copy.wait_recv()

    def fill(e_ref, nodes, width, slot):
        for i in range(width):
            lower = jnp.where(me == 0, 0.0, unpack(from_below[slot + i]))
            upper = jnp.where(me == devices - 1, 0.0, unpack(from_above[slot + i]))
            e_ref[i] = e_rows(lower)
            e_ref[nodes + width + i] = e_rows(upper)

    fill(e_ord, 64, 1, 0)
    fill(e0, 64, 3, 1)
    fill(e1, 32, 3, 4)
    fill(e2, 16, 3, 7)

    def partners(g, picks, blocks, e_ref, shift, result):
        for half in range(2):
            lhs, w = [], []
            for s in range(3):
                rows = []
                for n in range(4):
                    node = 8 * g + 4 * half + n
                    rows.append(e_ref[node + shift(picks[s, node])])
                lhs.append(jnp.concatenate(rows, axis=0))
                w.append(prepare(blocks.at[s], g, half))
            result[2 * g + half] = pick_diagonal(times(lhs, w))

    def near_shift(pick):
        return pick + 1

    def far_shift(pick):
        return pick + (pick >> 1) * 3

    def near_part(first):
        each(
            4,
            NEAR_UNROLL,
            lambda g: partners(g + first, near_pick, near_v, e_ord, near_shift, near_f),
        )

    def half_of(w_ref, g, half):
        return w_ref[g, :, 128 * half : 128 * half + 128]

    def times_wide(lhs, w):
        return dot_nt(lhs, jnp.concatenate([w, w], axis=1))

    def z_to_e(groups):
        def step(g):
            for half in range(2):
                q = 2 * g + half
                moved = dot(jnp.concatenate(split(z_d[q]), axis=0), to_n[...])
                for i in range(2):
                    at = slice(128 * i, 128 * i + 128)
                    heads, rests = pair(moved[0:64, at]), pair(moved[64:, at])
                    for k in range(2):
                        z_e[4 * q + 2 * i + k] = jnp.concatenate(
                            [heads[k].astype(BF16), rests[k].astype(BF16)], axis=1
                        )

        each(groups, Z_UNROLL, step)

    def compose_two():
        identity = jnp.where(iota((64, 64), 0) == iota((64, 64), 1), 1.0, 0.0).astype(F32)
        lift_t = dot_nt(identity, lift, EXACT)
        start = e_rows(jnp.concatenate([lift_t, lift_t], axis=1))
        for q in range(4):
            z_d[q] = times_wide(start, half_of(w_tr, q // 2, q % 2))
        z_to_e(2)

    def compose(groups, w_ref):
        def step(g):
            for half in range(2):
                q = 2 * g + half
                first, second = z_e[2 * q], z_e[2 * q + 1]
                lhs = jnp.concatenate([first, first, second, second], axis=0)
                z_d[q] = pick_diagonal(times_wide(lhs, half_of(w_ref, g, half)), 64)

        each(groups, Z_UNROLL, step)
        z_to_e(groups)

    def compose_leaves():
        def step(g):
            for half in range(2):
                q = 2 * g + half
                lhs = z_e[pl.ds(4 * q, 4)].reshape(256, 256)
                head, rest = split(
                    pick_diagonal(times_wide(lhs, half_of(w_lb, g, half)), 64)
                )
                z_w[q] = jnp.concatenate([head, rest, head, rest], axis=0)

        each(8, Z_UNROLL, step)

    def to_e(values, quads):
        moved = dot(jnp.concatenate(split(values), axis=0), to_n[...])
        rows = 16 * quads
        for q in range(quads):
            for i in range(2):
                at = slice(128 * i, 128 * i + 128)
                heads = pair(moved[16 * q : 16 * q + 16, at])
                rests = pair(moved[rows + 16 * q : rows + 16 * q + 16, at])
                for k in range(2):
                    e_down[4 * q + 2 * i + k] = jnp.concatenate(
                        [heads[k].astype(BF16), rests[k].astype(BF16)], axis=1
                    )

    def descend(groups, w_ref, far):
        def step(g):
            for half in range(2):
                q = 2 * g + half
                first, second = e_down[2 * q], e_down[2 * q + 1]
                lhs = jnp.concatenate([first, first, second, second], axis=0)
                far[q] = far[q] + pick_diagonal(times([lhs], [half_of(w_ref, g, half)]))

        each(groups, DOWN_UNROLL, step)
        to_e(jnp.concatenate([far[q] for q in range(2 * groups)], axis=0), 2 * groups)

    def leaf_down(g):
        for half in range(2):
            q = 2 * g + half
            lhs = e_down[pl.ds(4 * q, 4)].reshape(64, 256)
            near_f[q] = near_f[q] + pick_diagonal(times([lhs], [half_of(w_lb, g, half)]))

    over(1, 8, lambda q: a_copy(q).wait_recv())

    def total_of(buffer, slots):
        result = buffer[0]
        for q in range(1, slots):
            result = result + buffer[q]
        return result

    summed = total_of(a_buf, 8)
    b_send[...] = summed
    b_buf[group] = summed
    over(1, count, lambda q: b_copy(q).start())

    compose_two()
    compose(4, w_t2)
    compose(8, w_t1)
    loads["near"].wait()
    loads["tb"].wait()
    w_top = split_rows([tb_v[pl.ds(n, 32, stride=4), :] for n in range(4)])

    over(1, count, lambda q: b_arrival(q).wait_recv())

    picked = []
    for b in range(4):
        picked.append(e_rows(unpack(b_buf[top_source[b]])))
    coupled = pick_diagonal(times([jnp.concatenate(picked, axis=0)], [w_top]))
    moved = dot(jnp.concatenate(split(coupled), axis=0), to_n[...])
    moved = moved[0:16] + moved[16:32]
    packed = []
    for i in range(2):
        packed += [pack(block) for block in pair(moved[:, 128 * i : 128 * i + 128])]
    for q in range(count):
        target = group_at(q)
        part = jnp.zeros((8, 128), F32)
        for b in range(4):
            part = part + jnp.where(jnp.full((8, 128), top_target[b]) == target, packed[b], 0.0)
        if q == 0:
            c_buf[0] = part
        else:
            c_send[q] = part
    over(1, count, lambda q: c_copy(q).start())

    near_part(0)
    near_part(4)
    compose_leaves()
    loads["fc"].wait()
    each(2, NEAR_UNROLL, lambda g: partners(g, pick_c, fc_v, e2, far_shift, far_c))
    loads["fb"].wait()
    each(4, NEAR_UNROLL, lambda g: partners(g, pick_b, fb_v, e1, far_shift, far_b))
    loads["fa"].wait()
    each(8, NEAR_UNROLL, lambda g: partners(g, pick_a, fa_v, e0, far_shift, far_a))

    over(1, count, lambda q: c_copy(q).wait_recv())
    summed = total_of(c_buf, count)
    d_send[...] = summed
    d_buf[0] = summed
    over(1, 8, lambda q: d_copy(q).start())

    to_e(jnp.concatenate([far_c[q] for q in range(4)], axis=0), 4)
    descend(4, w_t2, far_b)
    descend(8, w_t1, far_a)
    each(8, DOWN_UNROLL, leaf_down)

    over(1, 8, lambda q: d_copy(q).wait_recv())
    falling = e_rows(unpack(total_of(d_buf, 8)))
    for q in range(16):
        value = near_f[q] + dot(falling, z_w[q])
        for i in range(2):
            vals[2 * q + i] = value[:, 128 * i : 128 * i + 128]

    up_copy.wait_send()
    down_copy.wait_send()
    over(1, 8, lambda q: a_copy(q).wait_send())
    over(1, count, lambda q: b_copy(q).wait_send())
    over(1, count, lambda q: c_copy(q).wait_send())
    over(1, 8, lambda q: d_copy(q).wait_send())


def restore(vals, inverse, out):
    table = table_of([vals[t] for t in range(32)])
    for j in range(8):
        rows = [inverse[4 * j + i : 4 * j + i + 1, :] for i in range(4)]
        lanes = [inverse[4 * j + i + 32 : 4 * j + i + 33, :] for i in range(4)]
        out[:, 512 * j : 512 * j + 512] = lookup(
            table, jnp.concatenate(rows, axis=1), jnp.concatenate(lanes, axis=1)
        )


def lay_out(flat):
    lead, nodes = flat.shape[:-2], flat.shape[-2]
    n = min(nodes, 8)
    rows = jnp.swapaxes(flat.reshape(lead + (nodes // n, n, 32, 128)), -3, -2)
    return rows.reshape(lead + (nodes * 32, 128))


def body(devices, *args):
    smem, hbm = pl.BlockSpec(memory_space=pltpu.SMEM), pl.BlockSpec(memory_space=pl.ANY)
    vm, whole = pltpu.VMEM, pl.BlockSpec(memory_space=pltpu.VMEM)
    args = [lay_out(a) if i in (2, 4, 5, 6, 7, 9, 11, 13, 14, 17) else a for i, a in enumerate(args)]
    small = (3, 8, 10, 12, 15, 16)
    count = devices // 8
    big = [0, 1, 2, 4, 5, 6, 7, 9, 11, 13, 14, 17]
    dma = pltpu.SemaphoreType.DMA
    scratch = [vm(args[i].shape, args[i].dtype) for i in big]
    scratch += [
        vm((8, 256, 256), BF16),
        vm((8, 256, 256), BF16),
        vm((4, 256, 256), BF16),
        vm((2, 256, 256), BF16),
        vm((256, 256), BF16),
        vm((256, 256), BF16),
        vm((64, 256), BF16),
        vm((2, 16, 16, 256), BF16),
        vm((512, 256), BF16),
        vm((32, 16, 128), F32),
        vm((66, 16, 256), BF16),
        vm((70, 16, 256), BF16),
        vm((38, 16, 256), BF16),
        vm((22, 16, 256), BF16),
        vm((64, 16, 256), BF16),
        vm((16, 64, 256), F32),
        vm((64, 64, 256), BF16),
        vm((16, 256, 256), BF16),
        vm((16, 16, 256), F32),
        vm((16, 16, 256), F32),
        vm((8, 16, 256), F32),
        vm((4, 16, 256), F32),
        vm((10, 8, 128), F32),
        vm((10, 8, 128), F32),
        vm((10, 8, 128), F32),
        vm((10, 8, 128), F32),
        vm((8, 128), F32),
        vm((8, 8, 128), F32),
        vm((8, 128), F32),
        vm((count, 8, 128), F32),
        vm((count, 8, 128), F32),
        vm((count, 8, 128), F32),
        vm((8, 128), F32),
        vm((8, 8, 128), F32),
        dma((12,)),
        dma((4,)),
        dma((8,)),
        dma((8,)),
        dma((count,)),
        dma((count,)),
        dma((count,)),
        dma((count,)),
        dma((8,)),
        dma((8,)),
    ]
    vals, inverse = pl.pallas_call(
        functools.partial(kernel, devices),
        out_shape=(
            jax.ShapeDtypeStruct((32, 16, 128), F32),
            jax.ShapeDtypeStruct((64, 128), I32),
        ),
        in_specs=[smem if i in small else hbm for i in range(18)],
        out_specs=(whole, whole),
        scratch_shapes=scratch,
        compiler_params=pltpu.CompilerParams(
            collective_id=0, has_side_effects=True, vmem_limit_bytes=60 * 1024 * 1024
        ),
    )(*args)
    return pl.pallas_call(
        restore,
        out_shape=jax.ShapeDtypeStruct((16, 4096), F32),
        in_specs=[whole] * 2,
        out_specs=whole,
        compiler_params=pltpu.CompilerParams(vmem_limit_bytes=60 * 1024 * 1024),
    )(vals, inverse)


def solution(mesh):
    split_rows, split_columns = P("leaf", None), P(None, "leaf")
    split_middle = P(None, "leaf", None)
    in_specs = (
        split_columns,
        split_rows,
        split_rows,
        split_columns,
        split_middle,
        split_rows,
        split_rows,
        split_rows,
        split_columns,
        split_middle,
        split_columns,
        split_middle,
        split_columns,
        split_middle,
        split_middle,
        P("leaf"),
        P("leaf"),
        split_rows,
    )
    return jax.shard_map(
        functools.partial(body, mesh.shape["leaf"]),
        mesh=mesh,
        in_specs=in_specs,
        out_specs=split_columns,
        check_vma=False,
    )
```
